128 devices in a mesh: row: 16 (over x, z), partner: 4 (over y), feat: 2 (over core).
Axes of the slice: x: 4, y: 4, z: 4, core: 2. Of those that a mesh axis runs over, the one named last changes fastest.
Arguments:
- embeddings: bfloat16 [1048576, 256], P(('row', 'partner'), 'feat'), may hold values from -1.5 to 1.5
- decoder_gain: float32 [256], P('feat'), may hold values from 0.5 to 2
- block_pairs: int32 [64, 64, 2, 2], replicated, may hold values from 0 to 8191, as said below
- pair_counts: int32 [64, 64], replicated, may hold values from 0 to 2, as said below
- edge_labels: bfloat16 [64, 64, 2, 128, 128], P(('row', 'partner')), may hold values from 0 to 1, as said below
Outputs:
- grad_embeddings: float32 [1048576, 256], P(('row', 'partner'), 'feat')
- grad_gain: float32 [256], P('feat')
The draws below stay inside these ranges and needn't reach their ends.
Inputs may be any that keep to these rules, and one draw needn't show every extreme that they name: pair_counts[r, o] is 0 for o < r, 2 for o = r and 1 to 2 for o > r. block_pairs[r, o, c, 0] is a block of requester r (r * 128 to (r + 1) * 128 - 1) and block_pairs[r, o, c, 1] a block of owner o; in live slots the row block is at most the column block. `edge_labels`: every entry is 0 or 1.
All inputs are finite; a program needn't handle non-finite values.
Results may differ from the reference program's by a relative error of at most 0.0044.
Values may be sent and summed in bfloat16 or wider, within the bound.
A program may use at most 128 MiB of HBM per device.

```python
import math
import jax
import jax.numpy as jnp
from jax import lax

E = 256
BLOCK = 128
BLK_DEV = 128
CAP = 2
NODE_OWNERS = 64
TOTAL_BLOCKS = 8192
NODES = 1048576


def draw_block_pairs(key, part):
    key_cols, key_rows = jax.random.split(jax.random.fold_in(key, 11))
    shape = (NODE_OWNERS, NODE_OWNERS, CAP)
    col_local = jax.random.randint(key_cols, shape, 0, BLK_DEV)
    raw_rows = jax.random.randint(key_rows, shape, 0, 1 << 20)
    requester_ids = jnp.arange(NODE_OWNERS)[:, None, None]
    owner_ids = jnp.arange(NODE_OWNERS)[None, :, None]
    row_limit = jnp.where(owner_ids > requester_ids, BLK_DEV, col_local + 1)
    row_local = raw_rows % row_limit
    row_blocks = requester_ids * BLK_DEV + row_local
    col_blocks = owner_ids * BLK_DEV + col_local
    return jnp.stack([row_blocks, col_blocks], axis=-1).astype(jnp.int32)


def draw_pair_counts(key, part):
    extra_count = jax.random.randint(jax.random.fold_in(key, 23), (NODE_OWNERS, NODE_OWNERS), 0, CAP)
    requester_ids = jnp.arange(NODE_OWNERS)[:, None]
    owner_ids = jnp.arange(NODE_OWNERS)[None, :]
    upper = jnp.where(owner_ids == requester_ids, CAP, 0)
    return jnp.where(owner_ids > requester_ids, 1 + extra_count, upper).astype(jnp.int32)


def draw_edge_labels(key, part):
    shape = (NODE_OWNERS, NODE_OWNERS, CAP, BLOCK, BLOCK)
    label_bits = jax.random.randint(jax.random.fold_in(key, 37), shape, 0, 2)
    return label_bits.astype(jnp.float32).astype(jnp.bfloat16)


def block_scale(rng, extent, cuts, low, top_value):
    def one(position, parts):
        heights = jax.random.uniform(jax.random.fold_in(jax.random.fold_in(rng, 6), position), (parts,), jnp.float32, low / len(cuts), top_value / len(cuts))
        return jnp.repeat(jnp.exp(heights), extent[position] // parts).reshape((-1,) + (1,) * (len(extent) - position - 1))

    factor_of = one(*cuts[0])
    for cut in cuts[1:]:
        factor_of = factor_of * one(*cut)
    return factor_of


def bell_draw(key, extent, deviation, reach, cuts=(), held_as=jnp.bfloat16):
    gain = block_scale(key, extent, cuts, -0.22, 0.18) if cuts else 1.0
    drawn = jax.random.normal(key, extent, jnp.float32) * deviation * gain
    return jnp.minimum(jnp.maximum(drawn, -reach), reach).astype(held_as)


def setup_inputs(seed: int = 0) -> dict:
    keys = jax.random.split(jax.random.key(seed), 6)
    embeddings = bell_draw(keys[0], (NODES, E), 0.25, 1.5, ((0, 64), (1, 2)))
    decoder_gain = jnp.clip(jnp.exp(math.log(2.0) - 1.3862944 * jax.random.uniform(keys[1], (E,), jnp.float32) ** block_scale(keys[1], (E,), ((0, 2),), -0.2, 0.2)), 0.5, 2.0)
    block_pairs = draw_block_pairs(jax.random.fold_in(keys[5], 71), 0)
    pair_counts = draw_pair_counts(jax.random.fold_in(keys[5], 71), 0)
    edge_labels = draw_edge_labels(jax.random.fold_in(keys[5], 71), 0)
    return dict(embeddings=embeddings, decoder_gain=decoder_gain, block_pairs=block_pairs, pair_counts=pair_counts, edge_labels=edge_labels)


def reference(embeddings, decoder_gain, block_pairs, pair_counts, edge_labels):
    blocks = embeddings.reshape(TOTAL_BLOCKS, BLOCK, E)
    scaled = (embeddings.astype(jnp.float32) * decoder_gain[None, :]).astype(jnp.bfloat16).reshape(TOTAL_BLOCKS, BLOCK, E)
    positions = jnp.arange(CAP)

    def per_requester(state_pair, requester):
        grad_sum, gain_part = state_pair
        my_pairs = lax.dynamic_index_in_dim(block_pairs, requester, 0, keepdims=False)
        rows_here = my_pairs[:, :, 0].reshape(-1).astype(jnp.int32)
        cols_here = my_pairs[:, :, 1].reshape(-1).astype(jnp.int32)
        have_count = lax.dynamic_index_in_dim(pair_counts, requester, 0, keepdims=False)
        live_mask = (positions[None, :] < have_count[:, None]).reshape(-1)
        target_tiles = lax.dynamic_index_in_dim(edge_labels, requester, 0, keepdims=False).reshape(-1, BLOCK, BLOCK)
        rows_in = blocks[rows_here].astype(jnp.float32)
        rows_scaled = scaled[rows_here].astype(jnp.float32)
        cols_in = blocks[cols_here].astype(jnp.float32)
        logits = jnp.einsum("sik,sjk->sij", rows_scaled, cols_in)
        residual = ((jax.nn.sigmoid(logits) - target_tiles.astype(jnp.float32)) * live_mask[:, None, None].astype(jnp.float32))
        residual = lax.optimization_barrier(residual.astype(jnp.bfloat16)).astype(jnp.float32)
        pulled = jnp.einsum("sij,sjk->sik", residual, cols_in)
        row_terms = lax.optimization_barrier((pulled * decoder_gain[None, None, :]).astype(jnp.bfloat16)).astype(jnp.float32)
        col_terms = jnp.einsum("sij,sik->sjk", residual, rows_scaled)
        col_terms = lax.optimization_barrier(col_terms.astype(jnp.bfloat16)).astype(jnp.float32)
        grad_sum = grad_sum.at[rows_here].add(row_terms)
        grad_sum = grad_sum.at[cols_here].add(col_terms)
        gain_part = gain_part + jnp.sum(rows_in * pulled, axis=(0, 1))
        return (grad_sum, gain_part), None

    initial = (jnp.zeros((TOTAL_BLOCKS, BLOCK, E), jnp.float32), jnp.zeros((E,), jnp.float32))
    (grad_sum, gain_part), _ = lax.scan(per_requester, initial, jnp.arange(NODE_OWNERS, dtype=jnp.int32))
    grad_gain = gain_part * (16.0 / (NODE_OWNERS * BLOCK))
    return grad_sum.reshape(NODES, E), grad_gain
```

```python
import functools

import jax
import jax.numpy as jnp
from jax import lax
from jax.experimental import pallas as pl
from jax.experimental.pallas import tpu as pltpu
from jax.sharding import PartitionSpec as P

GROUP = 4
NODE_SPLIT = 2
MESH = pl.DeviceIdType.MESH


def exchange_kernel(
    owners,
    partners,
    row_ids,
    col_ids,
    counts,
    gain_ref,
    emb_ref,
    labels_hbm,
    terms_hbm,
    gain_out,
    staged,
    cols,
    rows_send,
    rows_sib,
    labels,
    col_tiles,
    row_tiles,
    gains,
    gain_send,
    gain_sib,
    gain_all,
    col_send_sem,
    col_recv_sem,
    rows_send_sem,
    rows_recv_sem,
    label_sem,
    back_send_sem,
    row_send_sem,
    term_recv_sem,
    local_sem,
    small_send_sem,
    small_recv_sem,
    gain_send_sem,
    gain_recv_sem,
):
    groups = owners // GROUP
    me = lax.axis_index("row") * partners + lax.axis_index("partner")
    feat = lax.axis_index("feat")
    other = 1 - feat
    first_group = me // GROUP
    width = emb_ref.shape[-1]

    def device(chip, core):
        return (chip // partners, chip % partners, core)

    sibling = device(me, other)

    def remote(src, dst, send, recv, where):
        return pltpu.make_async_remote_copy(
            src_ref=src, dst_ref=dst, send_sem=send, recv_sem=recv,
            device_id=where, device_id_type=MESH,
        )

    def col_copy(chip, slot):
        return remote(
            staged.at[slot, chip], cols.at[me, feat], col_send_sem.at[slot, chip],
            col_recv_sem.at[me, feat], device(chip, slot),
        )

    def col_arrival(owner, half):
        return remote(
            staged.at[0, 0], cols.at[owner, half], col_send_sem.at[0, 0],
            col_recv_sem.at[owner, half], sibling,
        )

    def rows_copy(group):
        span = pl.ds(group * GROUP, GROUP)
        return remote(
            rows_send.at[span], rows_sib.at[span], rows_send_sem.at[group],
            rows_recv_sem.at[group], sibling,
        )

    def label_copy(group):
        span = pl.ds(group * GROUP, GROUP)
        return pltpu.make_async_copy(
            labels_hbm.at[span, feat], labels.at[span], label_sem.at[group]
        )

    def back_copy(owner, side):
        core = feat if side == 0 else other
        return remote(
            col_tiles.at[owner, side], terms_hbm.at[feat, me], back_send_sem.at[owner, side],
            term_recv_sem.at[feat, me], device(owner, core),
        )

    def back_own():
        return pltpu.make_async_copy(
            col_tiles.at[me, 0], terms_hbm.at[feat, me], local_sem.at[owners]
        )

    def row_own(owner):
        return pltpu.make_async_copy(
            row_tiles.at[owner, 0], terms_hbm.at[feat, owner + 1], local_sem.at[owner]
        )

    def row_copy(owner):
        return remote(
            row_tiles.at[owner, 1], terms_hbm.at[feat, owner + 1], row_send_sem.at[owner],
            term_recv_sem.at[feat, owner + 1], sibling,
        )

    def term_arrival(slot, place):
        return remote(
            col_tiles.at[0, 0], terms_hbm.at[slot, place], row_send_sem.at[0],
            term_recv_sem.at[slot, place], sibling,
        )

    gain_scale = remote(
        gain_ref, gains.at[feat], small_send_sem.at[0], small_recv_sem.at[0], sibling
    )
    gain_scale.start()
    gains[feat] = gain_ref[...]

    def send_cols(step, _):
        chip = me - step
        for slot in range(2):
            staged[slot, chip] = emb_ref[col_ids[slot, chip]]
            col_copy(chip, slot).start()
        return 0

    staged[other, me] = emb_ref[col_ids[other, me]]
    col_copy(me, other).start()
    cols[me, feat] = emb_ref[col_ids[feat, me]]
    lax.fori_loop(1, me + 1, send_cols, 0)

    def send_rows(group, _):
        label_copy(group).start()
        for j in range(GROUP):
            owner = group * GROUP + j
            rows_send[owner] = emb_ref[row_ids[other, owner]]
        rows_copy(group).start()
        return 0

    lax.fori_loop(first_group, groups, send_rows, 0)

    gain_scale.wait_recv()
    gain_pair = jnp.concatenate([gains[feat], gains[other]], axis=-1)[:1]

    def work(group, gain_sum):
        rows_copy(group).wait_recv()
        label_copy(group).wait()
        for j in range(GROUP):
            owner = group * GROUP + j

            @pl.when(owner > me)
            def _():
                col_arrival(owner, feat).wait_recv()

            @pl.when(owner >= me)
            def _():
                col_arrival(owner, other).wait_recv()

        for j in range(GROUP):
            owner = group * GROUP + j
            source = jnp.maximum(owner, me)
            live = jnp.where(feat < counts[owner], 1.0, 0.0)
            rows = jnp.concatenate([emb_ref[row_ids[feat, owner]], rows_sib[owner]], axis=-1)
            rows_wide = rows.astype(jnp.float32)
            scaled = (rows_wide * gain_pair).astype(jnp.bfloat16)
            col = jnp.concatenate([cols[source, feat], cols[source, other]], axis=-1)
            logits = lax.dot_general(
                scaled, col, (((1,), (1,)), ((), ())), preferred_element_type=jnp.float32
            )
            prob = 0.5 * jnp.tanh(0.5 * logits) + 0.5
            residual = ((prob - labels[owner].astype(jnp.float32)) * live).astype(jnp.bfloat16)
            pulled = jnp.dot(residual, col, preferred_element_type=jnp.float32)
            row_term = (pulled * gain_pair).astype(jnp.bfloat16)
            col_term = lax.dot_general(
                residual, scaled, (((0,), (0,)), ((), ())), preferred_element_type=jnp.float32
            ).astype(jnp.bfloat16)
            col_tiles[owner, 0] = col_term[:, :width]
            col_tiles[owner, 1] = col_term[:, width:]
            row_tiles[owner, 0] = row_term[:, :width]
            row_tiles[owner, 1] = row_term[:, width:]
            product = rows_wide * pulled
            gain_sum = gain_sum + jnp.sum(product.reshape(-1, 8, 2 * width), axis=0)

        for j in range(GROUP):
            owner = group * GROUP + j

            @pl.when(owner > me)
            def _():
                back_copy(owner, 0).start()

            @pl.when(owner == me)
            def _():
                back_own().start()

            @pl.when(owner >= me)
            def _():
                back_copy(owner, 1).start()
                row_copy(owner).start()
                row_own(owner).start()

        return gain_sum

    gain_sum = lax.fori_loop(
        first_group, groups, work, jnp.zeros((8, 2 * width), jnp.float32)
    )

    gain_send[0] = gain_sum[:, width:]
    gain_pairwise = remote(
        gain_send.at[0], gain_sib, small_send_sem.at[1], small_recv_sem.at[1], sibling
    )
    gain_pairwise.start()
    gain_pairwise.wait_recv()
    chip_gain = jnp.sum(gain_sum[:, :width] + gain_sib[...], axis=0, keepdims=True)
    chip_gain = jnp.broadcast_to(chip_gain, (8, width))
    gain_send[1] = chip_gain
    gain_all[me] = chip_gain

    def gain_copy(step):
        chip = lax.rem(me + step, owners)
        return remote(
            gain_send.at[1], gain_all.at[me], gain_send_sem.at[chip],
            gain_recv_sem.at[me], device(chip, feat),
        )

    def gain_arrival(step):
        chip = lax.rem(me + step, owners)
        return remote(
            gain_send.at[1], gain_all.at[chip], gain_send_sem.at[chip],
            gain_recv_sem.at[chip], device(chip, feat),
        )

    def start_gain(step, _):
        gain_copy(step).start()
        return 0

    lax.fori_loop(1, owners, start_gain, 0)

    def wait_gain(step, _):
        gain_arrival(step).wait_recv()
        gain_copy(step).wait_send()
        return 0

    lax.fori_loop(1, owners, wait_gain, 0)

    def add_gain(chip, total):
        return total + gain_all[chip]

    total = lax.fori_loop(0, owners, add_gain, jnp.zeros((8, width), jnp.float32))
    gain_out[...] = total * (16.0 / (owners * emb_ref.shape[1]))

    def drain_cols(step, _):
        chip = me - step
        for slot in range(2):
            col_copy(chip, slot).wait_send()
            term_arrival(slot, chip).wait_recv()
        return 0

    lax.fori_loop(1, me + 1, drain_cols, 0)
    col_copy(me, other).wait_send()
    term_arrival(other, me).wait_recv()
    back_own().wait()

    def drain_rows(group, _):
        rows_copy(group).wait_send()
        return 0

    lax.fori_loop(first_group, groups, drain_rows, 0)

    def drain_back(owner, _):
        back_copy(owner, 1).wait_send()
        row_copy(owner).wait_send()
        row_own(owner).wait()
        term_arrival(other, owner + 1).wait_recv()
        return 0

    lax.fori_loop(me, owners, drain_back, 0)

    def drain_back_own(owner, _):
        back_copy(owner, 0).wait_send()
        return 0

    lax.fori_loop(me + 1, owners, drain_back_own, 0)
    gain_scale.wait_send()
    gain_pairwise.wait_send()


def add_kernel(ids, terms_ref, out_ref):
    out_ref[...] = jnp.zeros_like(out_ref)
    places = terms_ref.shape[1]

    def add(place, _):
        for slot in range(2):
            block = ids[slot, place]
            out_ref[block] += terms_ref[slot, place].astype(jnp.float32)
        return 0

    lax.fori_loop(0, places, add, 0)


def local(embeddings, decoder_gain, block_pairs, pair_counts, edge_labels):
    partners = lax.axis_size("partner")
    owners = lax.axis_size("row") * partners
    me = lax.axis_index(("row", "partner"))
    tile = edge_labels.shape[-1]
    width = embeddings.shape[1]
    blocks = embeddings.shape[0] // tile
    resident = embeddings.reshape(blocks, tile, width)
    labels = edge_labels.reshape(owners, 2, tile, tile)
    base = me * blocks
    as_requester = lax.dynamic_index_in_dim(block_pairs, me, 0, keepdims=False)
    as_owner = lax.dynamic_index_in_dim(block_pairs, me, 1, keepdims=False)
    row_ids = (as_requester[:, :, 0] - base).T
    col_ids = (as_owner[:, :, 1] - base).T
    counts = lax.dynamic_index_in_dim(pair_counts, me, 0, keepdims=False)
    place = jnp.arange(owners + 1)[None, :]
    ids = jnp.where(
        place <= me,
        jnp.pad(col_ids, ((0, 0), (0, 1))),
        jnp.pad(row_ids, ((0, 0), (1, 0))),
    )
    gain_rows = jnp.broadcast_to(decoder_gain[None, :], (8, width))

    smem = pl.BlockSpec(memory_space=pltpu.SMEM)
    vmem = pl.BlockSpec(memory_space=pltpu.VMEM)
    anywhere = pl.BlockSpec(memory_space=pl.ANY)
    dma = pltpu.SemaphoreType.DMA
    half = jnp.bfloat16
    groups = owners // GROUP
    terms, gain_total = pl.pallas_call(
        functools.partial(exchange_kernel, owners, partners),
        out_shape=(
            jax.ShapeDtypeStruct((2, owners + 1, tile, width), half),
            jax.ShapeDtypeStruct((8, width), jnp.float32),
        ),
        in_specs=[smem, smem, smem, vmem, vmem, anywhere],
        out_specs=(anywhere, vmem),
        scratch_shapes=[
            pltpu.VMEM((2, owners, tile, width), half),
            pltpu.VMEM((owners, 2, tile, width), half),
            pltpu.VMEM((owners, tile, width), half),
            pltpu.VMEM((owners, tile, width), half),
            pltpu.VMEM((owners, tile, tile), half),
            pltpu.VMEM((owners, 2, tile, width), half),
            pltpu.VMEM((owners, 2, tile, width), half),
            pltpu.VMEM((2, 8, width), jnp.float32),
            pltpu.VMEM((2, 8, width), jnp.float32),
            pltpu.VMEM((8, width), jnp.float32),
            pltpu.VMEM((owners, 8, width), jnp.float32),
            dma((2, owners)),
            dma((owners, 2)),
            dma((groups,)),
            dma((groups,)),
            dma((groups,)),
            dma((owners, 2)),
            dma((owners,)),
            dma((2, owners + 1)),
            dma((owners + 1,)),
            dma((2,)),
            dma((2,)),
            dma((owners,)),
            dma((owners,)),
        ],
        compiler_params=pltpu.CompilerParams(
            has_side_effects=True, vmem_limit_bytes=48 * 2**20
        ),
        name="exchange",
    )(row_ids, col_ids, counts, gain_rows, resident, labels)

    part = tile // NODE_SPLIT
    grad = pl.pallas_call(
        add_kernel,
        grid_spec=pltpu.PrefetchScalarGridSpec(
            num_scalar_prefetch=1,
            grid=(NODE_SPLIT,),
            in_specs=[pl.BlockSpec((2, owners + 1, part, width), lambda i, ids: (0, 0, i, 0))],
            out_specs=pl.BlockSpec((blocks, part, width), lambda i, ids: (0, i, 0)),
        ),
        out_shape=jax.ShapeDtypeStruct((blocks, tile, width), jnp.float32),
        compiler_params=pltpu.CompilerParams(vmem_limit_bytes=48 * 2**20),
        name="add_terms",
    )(ids, terms)
    return grad.reshape(blocks * tile, width), gain_total[0]


def solution(mesh):
    in_specs = (
        P(("row", "partner"), "feat"),
        P("feat"),
        P(),
        P(),
        P(("row", "partner"), None, None, None, None),
    )
    out_specs = (P(("row", "partner"), "feat"), P("feat"))
    return jax.shard_map(local, mesh=mesh, in_specs=in_specs, out_specs=out_specs, check_vma=False)
```

```python
import functools

import jax
import jax.numpy as jnp
from jax import lax
from jax.experimental import pallas as pl
from jax.experimental.pallas import tpu as pltpu
from jax.sharding import PartitionSpec as P

NODE_SPLIT = 2
MESH = pl.DeviceIdType.MESH


def exchange_kernel(
    chips,
    span,
    sent_ids,
    kept_ids,
    diagonal_ids,
    live,
    gain_ref,
    emb_hbm,
    labels_hbm,
    terms_hbm,
    gain_out,
    emb,
    staged,
    staged_sib,
    blocks,
    labels,
    grads,
    gains,
    gain_send,
    gain_sib,
    gain_all,
    emb_sem,
    block_send_sem,
    block_recv_sem,
    label_send_sem,
    label_recv_sem,
    label_own_sem,
    sib_send_sem,
    sib_recv_sem,
    back_send_sem,
    keep_send_sem,
    keep_own_sem,
    term_recv_sem,
    small_send_sem,
    small_recv_sem,
    gain_send_sem,
    gain_recv_sem,
):
    row = lax.axis_index("row")
    x, y, z = row // span, lax.axis_index("partner"), row % span
    me = row * span + y
    feat = lax.axis_index("feat")
    other = 1 - feat
    width = emb.shape[-1]
    half_rows = labels.shape[1] // 2
    my_rows = pl.ds(pl.multiple_of(feat * half_rows, half_rows), half_rows)

    def place(chip, core):
        return (chip // span, chip % span, core)

    sibling = place(me, other)

    def remote(src, dst, send, recv, where):
        return pltpu.make_async_remote_copy(
            src_ref=src, dst_ref=dst, send_sem=send, recv_sem=recv,
            device_id=where, device_id_type=MESH,
        )

    def shifted(step, sign):
        d = step % span
        b = (step // span) % span
        c = step // (span * span)
        dx = (d + b) % span
        px = (x + sign * dx + span) % span
        py = (y + sign * ((d + c) % span) + span) % span
        pz = (z + sign * d + span) % span
        return (px * span + pz) * span + py, dx % 2

    def kept_role(peer):
        return jnp.where(peer < me, 1, 0)

    def block_copy(peer, core):
        role = jnp.where(peer > me, 0, 1)
        return remote(
            staged.at[peer], blocks.at[me, role, feat], block_send_sem.at[peer],
            block_recv_sem.at[me, feat], place(peer, core),
        )

    def block_arrival(peer, half):
        return remote(
            staged.at[peer], blocks.at[peer, 1 - kept_role(peer), half], block_send_sem.at[peer],
            block_recv_sem.at[peer, half], sibling,
        )

    def label_copy(peer, core):
        return remote(
            labels_hbm.at[peer, 1, my_rows], labels.at[me, my_rows], label_send_sem.at[peer],
            label_recv_sem.at[me, feat], place(peer, core),
        )

    def label_arrival(peer, half):
        return remote(
            labels_hbm.at[peer, 1, pl.ds(half * half_rows, half_rows)],
            labels.at[peer, pl.ds(half * half_rows, half_rows)],
            label_send_sem.at[peer], label_recv_sem.at[peer, half], sibling,
        )

    def label_own(peer, slot):
        return pltpu.make_async_copy(
            labels_hbm.at[peer, slot], labels.at[peer], label_own_sem.at[peer]
        )

    def sib_copy(peer):
        return remote(
            staged_sib.at[peer], blocks.at[peer, kept_role(peer), feat], sib_send_sem.at[peer],
            sib_recv_sem.at[peer], sibling,
        )

    def sib_arrival(peer):
        return remote(
            staged_sib.at[peer], blocks.at[peer, kept_role(peer), other], sib_send_sem.at[peer],
            sib_recv_sem.at[peer], sibling,
        )

    def diagonal_col_copy():
        return remote(
            staged.at[me], blocks.at[me, 1, feat], block_send_sem.at[me],
            block_recv_sem.at[me, feat], sibling,
        )

    def diagonal_col_arrival():
        return remote(
            staged.at[me], blocks.at[me, 1, other], block_send_sem.at[me],
            block_recv_sem.at[me, other], sibling,
        )

    def back_copy(peer, half):
        return remote(
            grads.at[peer, 1 - kept_role(peer), half], terms_hbm.at[0, me],
            back_send_sem.at[peer, half], term_recv_sem.at[0, me], place(peer, half),
        )

    def keep_copy(peer):
        return remote(
            grads.at[peer, kept_role(peer), other], terms_hbm.at[1, peer],
            keep_send_sem.at[peer], term_recv_sem.at[1, peer], sibling,
        )

    def keep_own(peer):
        return pltpu.make_async_copy(
            grads.at[peer, kept_role(peer), feat], terms_hbm.at[1, peer], keep_own_sem.at[peer]
        )

    def diagonal_copy(role):
        where = me if role == 0 else chips
        return remote(
            grads.at[me, role, other], terms_hbm.at[feat, where],
            back_send_sem.at[me, role], term_recv_sem.at[feat, where], sibling,
        )

    def diagonal_own(role):
        where = me if role == 0 else chips
        return pltpu.make_async_copy(
            grads.at[me, role, feat], terms_hbm.at[feat, where], keep_own_sem.at[chips - role * chips + role * me]
        )

    def term_arrival(kind, where):
        return remote(
            staged.at[0], terms_hbm.at[kind, where], keep_send_sem.at[0],
            term_recv_sem.at[kind, where], sibling,
        )

    emb_copy = pltpu.make_async_copy(emb_hbm, emb, emb_sem.at[0])
    emb_copy.start()
    barrier = pltpu.get_barrier_semaphore()
    pl.semaphore_signal(barrier, 1, device_id=sibling, device_id_type=MESH)

    def greet(step, _):
        peer = lax.rem(me + step, chips)
        for core in range(2):
            pl.semaphore_signal(barrier, 1, device_id=place(peer, core), device_id_type=MESH)
        return 0

    lax.fori_loop(1, chips, greet, 0)
    label_own(me, feat).start()

    def load_labels(step, _):
        peer, core = shifted(step, -1)

        @pl.when((core == feat) & (peer > me))
        def _():
            label_own(peer, 0).start()

        return 0

    lax.fori_loop(1, chips, load_labels, 0)
    emb_copy.wait()

    def stage(step, _):
        peer, core = shifted(step, 1)
        staged[peer] = emb[sent_ids[peer]]

        @pl.when(core == feat)
        def _():
            blocks[peer, kept_role(peer), feat] = emb[kept_ids[peer]]

        @pl.when(core == other)
        def _():
            staged_sib[peer] = emb[kept_ids[peer]]

        return 0

    lax.fori_loop(1, chips, stage, 0)
    staged_sib[me] = emb[diagonal_ids[other, 0]]
    staged[me] = emb[diagonal_ids[other, 1]]
    blocks[me, 0, feat] = emb[diagonal_ids[feat, 0]]
    blocks[me, 1, feat] = emb[diagonal_ids[feat, 1]]
    gains[feat] = gain_ref[...]

    pl.semaphore_wait(barrier, 2 * chips - 1)
    gain_scale = remote(
        gain_ref, gains.at[feat], small_send_sem.at[0], small_recv_sem.at[0], sibling
    )
    gain_scale.start()
    sib_copy(me).start()
    diagonal_col_copy().start()

    def send(step, _):
        peer, core = shifted(step, 1)
        block_copy(peer, core).start()

        @pl.when(peer > me)
        def _():
            label_copy(peer, core).start()

        mirror, core_mirror = shifted(step, -1)

        @pl.when(core_mirror == other)
        def _():
            sib_copy(mirror).start()

        return 0

    lax.fori_loop(1, chips, send, 0)

    gain_scale.wait_recv()
    gain_pair = jnp.concatenate([gains[feat], gains[other]], axis=-1)[:1]

    def tile(peer, goes_to, is_live, gain_sum):
        rows = jnp.concatenate([blocks[peer, 0, feat], blocks[peer, 0, other]], axis=-1)
        col = jnp.concatenate([blocks[peer, 1, feat], blocks[peer, 1, other]], axis=-1)
        rows_wide = rows.astype(jnp.float32)
        scaled = (rows_wide * gain_pair).astype(jnp.bfloat16)
        logits = lax.dot_general(
            scaled, col, (((1,), (1,)), ((), ())), preferred_element_type=jnp.float32
        )
        prob = 0.5 * jnp.tanh(0.5 * logits) + 0.5
        residual = ((prob - labels[peer].astype(jnp.float32)) * is_live).astype(jnp.bfloat16)
        pulled = jnp.dot(residual, col, preferred_element_type=jnp.float32)
        row_term = (pulled * gain_pair).astype(jnp.bfloat16)
        col_term = lax.dot_general(
            residual, scaled, (((0,), (0,)), ((), ())), preferred_element_type=jnp.float32
        ).astype(jnp.bfloat16)
        grads[goes_to, 0, feat] = row_term[:, :width]
        grads[goes_to, 0, other] = row_term[:, width:]
        grads[goes_to, 1, feat] = col_term[:, :width]
        grads[goes_to, 1, other] = col_term[:, width:]
        product = rows_wide * pulled
        return gain_sum + jnp.sum(product.reshape(-1, 8, 2 * width), axis=0)

    sib_arrival(me).wait_recv()
    diagonal_col_arrival().wait_recv()
    label_own(me, feat).wait()
    gain_sum = tile(
        me, me, jnp.where(live[me] > feat, 1.0, 0.0), jnp.zeros((8, 2 * width), jnp.float32)
    )
    for role in range(2):
        diagonal_copy(role).start()
        diagonal_own(role).start()

    def mine(group, j):
        window = 2 * group + j // (span // 2)
        d = (feat + window) % 2 + 2 * (j % (span // 2))
        return shifted(window * span + d, -1)[0]

    def work(group, gain_sum):
        peers = [mine(group, j) for j in range(span)]
        for peer in peers:

            @pl.when(peer != me)
            def _(peer=peer):
                sib_arrival(peer).wait_recv()
                for half in range(2):
                    block_arrival(peer, half).wait_recv()

            @pl.when(peer > me)
            def _(peer=peer):
                label_own(peer, 0).wait()

            @pl.when(peer < me)
            def _(peer=peer):
                for half in range(2):
                    label_arrival(peer, half).wait_recv()

        for peer in peers:
            is_live = jnp.where(live[peer] > 0, 1.0, 0.0)
            is_live = jnp.where(peer == me, 0.0, is_live)
            gain_sum = tile(peer, jnp.where(peer == me, chips, peer), is_live, gain_sum)
        for peer in peers:

            @pl.when(peer != me)
            def _(peer=peer):
                for half in range(2):
                    back_copy(peer, half).start()
                keep_copy(peer).start()
                keep_own(peer).start()

        return gain_sum

    gain_sum = lax.fori_loop(0, chips // (2 * span), work, gain_sum)

    gain_send[0] = gain_sum[:, width:]
    gain_pairwise = remote(
        gain_send.at[0], gain_sib, small_send_sem.at[1], small_recv_sem.at[1], sibling
    )
    gain_pairwise.start()
    gain_pairwise.wait_recv()
    chip_gain = jnp.sum(gain_sum[:, :width] + gain_sib[...], axis=0, keepdims=True)
    chip_gain = jnp.broadcast_to(chip_gain, (8, width))
    gain_send[1] = chip_gain
    gain_all[me] = chip_gain

    def gain_copy(peer):
        return remote(
            gain_send.at[1], gain_all.at[me], gain_send_sem.at[peer],
            gain_recv_sem.at[me], place(peer, feat),
        )

    def gain_arrival(peer):
        return remote(
            gain_send.at[1], gain_all.at[peer], gain_send_sem.at[peer],
            gain_recv_sem.at[peer], sibling,
        )

    def start_gain(step, _):
        gain_copy(shifted(step, 1)[0]).start()
        return 0

    lax.fori_loop(1, chips, start_gain, 0)

    def drain(step, _):
        peer, core = shifted(step, 1)
        block_copy(peer, core).wait_send()

        @pl.when(peer > me)
        def _():
            label_copy(peer, core).wait_send()

        term_arrival(0, peer).wait_recv()

        @pl.when(core == other)
        def _():
            sib_copy(peer).wait_send()
            term_arrival(1, peer).wait_recv()

        @pl.when(core == feat)
        def _():
            for half in range(2):
                back_copy(peer, half).wait_send()
            keep_copy(peer).wait_send()
            keep_own(peer).wait()

        return 0

    lax.fori_loop(1, chips, drain, 0)

    def wait_gain(step, _):
        peer = shifted(step, 1)[0]
        gain_arrival(peer).wait_recv()
        gain_copy(peer).wait_send()
        return 0

    lax.fori_loop(1, chips, wait_gain, 0)

    def add_gain(chip, total):
        return total + gain_all[chip]

    total = lax.fori_loop(0, chips, add_gain, jnp.zeros((8, width), jnp.float32))
    gain_out[...] = total * (16.0 / (chips * emb.shape[1]))

    for role in range(2):
        diagonal_copy(role).wait_send()
        diagonal_own(role).wait()
        term_arrival(other, me if role == 0 else chips).wait_recv()
    sib_copy(me).wait_send()
    diagonal_col_copy().wait_send()
    gain_scale.wait_send()
    gain_pairwise.wait_send()


def add_kernel(ids, terms_ref, out_ref):
    out_ref[...] = jnp.zeros_like(out_ref)
    places = terms_ref.shape[1]

    def add(where, _):
        for slot in range(2):
            block = ids[slot, where]
            out_ref[block] += terms_ref[slot, where].astype(jnp.float32)
        return 0

    lax.fori_loop(0, places, add, 0)


def local(embeddings, decoder_gain, block_pairs, pair_counts, edge_labels):
    span = lax.axis_size("partner")
    chips = lax.axis_size("row") * span
    me = lax.axis_index(("row", "partner"))
    tile = edge_labels.shape[-1]
    width = embeddings.shape[1]
    count = embeddings.shape[0] // tile
    resident = embeddings.reshape(count, tile, width)
    labels = edge_labels.reshape(chips, 2, tile, tile)
    base = me * count
    row_ids = lax.dynamic_index_in_dim(block_pairs, me, 0, keepdims=False)[:, :, 0] - base
    col_ids = lax.dynamic_index_in_dim(block_pairs, me, 1, keepdims=False)[:, :, 1] - base
    as_requester = lax.dynamic_index_in_dim(pair_counts, me, 0, keepdims=False)
    as_owner = lax.dynamic_index_in_dim(pair_counts, me, 1, keepdims=False)
    peers = jnp.arange(chips)
    sent_ids = jnp.where(peers > me, row_ids[:, 1], col_ids[:, 0])
    kept_ids = jnp.where(peers > me, row_ids[:, 0], col_ids[:, 1])
    live = jnp.where(peers < me, as_owner - 1, as_requester)
    diagonal_ids = jnp.stack(
        [
            lax.dynamic_index_in_dim(row_ids, me, 0, keepdims=False),
            lax.dynamic_index_in_dim(col_ids, me, 0, keepdims=False),
        ],
        axis=1,
    )
    ids = jnp.where(peers == me, diagonal_ids[:, :1], jnp.stack([sent_ids, kept_ids]))
    ids = jnp.concatenate([ids, diagonal_ids[:, 1:]], axis=1)
    gain_rows = jnp.broadcast_to(decoder_gain[None, :], (8, width))

    smem = pl.BlockSpec(memory_space=pltpu.SMEM)
    vmem = pl.BlockSpec(memory_space=pltpu.VMEM)
    anywhere = pl.BlockSpec(memory_space=pl.ANY)
    dma = pltpu.SemaphoreType.DMA
    half = jnp.bfloat16
    terms, gain_total = pl.pallas_call(
        functools.partial(exchange_kernel, chips, span),
        out_shape=(
            jax.ShapeDtypeStruct((2, chips + 1, tile, width), half),
            jax.ShapeDtypeStruct((8, width), jnp.float32),
        ),
        in_specs=[smem, smem, smem, smem, vmem, anywhere, anywhere],
        out_specs=(anywhere, vmem),
        scratch_shapes=[
            pltpu.VMEM((count, tile, width), half),
            pltpu.VMEM((chips, tile, width), half),
            pltpu.VMEM((chips, tile, width), half),
            pltpu.VMEM((chips, 2, 2, tile, width), half),
            pltpu.VMEM((chips, tile, tile), half),
            pltpu.VMEM((chips + 1, 2, 2, tile, width), half),
            pltpu.VMEM((2, 8, width), jnp.float32),
            pltpu.VMEM((2, 8, width), jnp.float32),
            pltpu.VMEM((8, width), jnp.float32),
            pltpu.VMEM((chips, 8, width), jnp.float32),
            dma((1,)),
            dma((chips,)),
            dma((chips, 2)),
            dma((chips,)),
            dma((chips, 2)),
            dma((chips,)),
            dma((chips,)),
            dma((chips,)),
            dma((chips, 2)),
            dma((chips,)),
            dma((chips + 1,)),
            dma((2, chips + 1)),
            dma((2,)),
            dma((2,)),
            dma((chips,)),
            dma((chips,)),
        ],
        compiler_params=pltpu.CompilerParams(
            collective_id=0, has_side_effects=True, vmem_limit_bytes=56 * 2**20
        ),
        name="exchange",
    )(sent_ids, kept_ids, diagonal_ids, live, gain_rows, resident, labels)

    part = tile // NODE_SPLIT
    grad = pl.pallas_call(
        add_kernel,
        grid_spec=pltpu.PrefetchScalarGridSpec(
            num_scalar_prefetch=1,
            grid=(NODE_SPLIT,),
            in_specs=[pl.BlockSpec((2, chips + 1, part, width), lambda i, ids: (0, 0, i, 0))],
            out_specs=pl.BlockSpec((count, part, width), lambda i, ids: (0, i, 0)),
        ),
        out_shape=jax.ShapeDtypeStruct((count, tile, width), jnp.float32),
        compiler_params=pltpu.CompilerParams(vmem_limit_bytes=48 * 2**20),
        name="add_terms",
    )(ids, terms)
    return grad.reshape(count * tile, width), gain_total[0]


def solution(mesh):
    in_specs = (
        P(("row", "partner"), "feat"),
        P("feat"),
        P(),
        P(),
        P(("row", "partner"), None, None, None, None),
    )
    out_specs = (P(("row", "partner"), "feat"), P("feat"))
    return jax.shard_map(local, mesh=mesh, in_specs=in_specs, out_specs=out_specs, check_vma=False)
```

```python
import functools

import jax
import jax.numpy as jnp
from jax import lax
from jax.experimental import pallas as pl
from jax.experimental.pallas import tpu as pltpu
from jax.sharding import PartitionSpec as P

NODE_SPLIT = 2
MESH = pl.DeviceIdType.MESH


def exchange_kernel(
    chips,
    span,
    gain_ref,
    pairs_hbm,
    counts_hbm,
    emb_hbm,
    labels_hbm,
    terms_hbm,
    gain_out,
    ids_out,
    pairs,
    counts,
    emb,
    staged,
    staged_sib,
    blocks,
    labels,
    grads,
    gains,
    gain_send,
    gain_sib,
    gain_all,
    entry_sem,
    block_send_sem,
    block_recv_sem,
    label_send_sem,
    label_recv_sem,
    label_own_sem,
    sib_send_sem,
    sib_recv_sem,
    back_send_sem,
    keep_send_sem,
    keep_own_sem,
    term_recv_sem,
    small_send_sem,
    small_recv_sem,
    gain_send_sem,
    gain_recv_sem,
):
    row = lax.axis_index("row")
    x, y, z = row // span, lax.axis_index("partner"), row % span
    me = row * span + y
    feat = lax.axis_index("feat")
    other = 1 - feat
    width = emb.shape[-1]
    half_rows = labels.shape[1] // 2
    my_rows = pl.ds(pl.multiple_of(feat * half_rows, half_rows), half_rows)

    def place(chip, core):
        return (chip // span, chip % span, core)

    sibling = place(me, other)

    def remote(src, dst, send, recv, where):
        return pltpu.make_async_remote_copy(
            src_ref=src, dst_ref=dst, send_sem=send, recv_sem=recv,
            device_id=where, device_id_type=MESH,
        )

    count = emb.shape[0]
    base = me * count

    def resident(block):
        return jnp.clip(block - base, 0, count - 1)

    def sent_id(peer):
        return resident(jnp.where(peer > me, pairs[me, 1, 0, peer], pairs[peer, 0, 1, me]))

    def kept_id(peer):
        return resident(jnp.where(peer > me, pairs[me, 0, 0, peer], pairs[peer, 1, 1, me]))

    def diagonal_id(slot, role):
        return resident(pairs[me, slot, role, me])

    def window_step(window, d, sign):
        b, c = lax.rem(window, span), lax.div(window, span)
        dx, dy = lax.rem(d + b, span), lax.rem(d + c, span)
        if sign < 0:
            dx, dy, d = span - dx, span - dy, span - d
        px, py, pz = lax.rem(x + dx, span), lax.rem(y + dy, span), lax.rem(z + d, span)
        return (px * span + pz) * span + py, lax.rem(dx, 2)

    def kept_role(peer):
        return jnp.where(peer < me, 1, 0)

    def block_copy(peer, core):
        role = jnp.where(peer > me, 0, 1)
        return remote(
            staged.at[peer], blocks.at[me, role, feat], block_send_sem.at[peer],
            block_recv_sem.at[me, feat], place(peer, core),
        )

    def block_arrival(peer, half):
        return remote(
            staged.at[peer], blocks.at[peer, 1 - kept_role(peer), half], block_send_sem.at[peer],
            block_recv_sem.at[peer, half], sibling,
        )

    def label_copy(peer, core):
        return remote(
            labels_hbm.at[peer, 1, my_rows], labels.at[me, my_rows], label_send_sem.at[peer],
            label_recv_sem.at[me, feat], place(peer, core),
        )

    def label_arrival(peer, half):
        return remote(
            labels_hbm.at[peer, 1, pl.ds(half * half_rows, half_rows)],
            labels.at[peer, pl.ds(half * half_rows, half_rows)],
            label_send_sem.at[peer], label_recv_sem.at[peer, half], sibling,
        )

    def label_own(peer, slot):
        return pltpu.make_async_copy(
            labels_hbm.at[peer, slot], labels.at[peer], label_own_sem.at[peer]
        )

    def sib_copy(peer):
        return remote(
            staged_sib.at[peer], blocks.at[peer, kept_role(peer), feat], sib_send_sem.at[peer],
            sib_recv_sem.at[peer], sibling,
        )

    def sib_arrival(peer):
        return remote(
            staged_sib.at[peer], blocks.at[peer, kept_role(peer), other], sib_send_sem.at[peer],
            sib_recv_sem.at[peer], sibling,
        )

    def diagonal_col_copy():
        return remote(
            staged.at[me], blocks.at[me, 1, feat], block_send_sem.at[me],
            block_recv_sem.at[me, feat], sibling,
        )

    def diagonal_col_arrival():
        return remote(
            staged.at[me], blocks.at[me, 1, other], block_send_sem.at[me],
            block_recv_sem.at[me, other], sibling,
        )

    def back_copy(peer, half):
        return remote(
            grads.at[peer, 1 - kept_role(peer), half], terms_hbm.at[0, me],
            back_send_sem.at[peer, half], term_recv_sem.at[0, me], place(peer, half),
        )

    def keep_copy(peer):
        return remote(
            grads.at[peer, kept_role(peer), other], terms_hbm.at[1, peer],
            keep_send_sem.at[peer], term_recv_sem.at[1, peer], sibling,
        )

    def keep_own(peer):
        return pltpu.make_async_copy(
            grads.at[peer, kept_role(peer), feat], terms_hbm.at[1, peer], keep_own_sem.at[peer]
        )

    def diagonal_copy(role):
        where = me if role == 0 else chips
        return remote(
            grads.at[me, role, other], terms_hbm.at[feat, where],
            back_send_sem.at[me, role], term_recv_sem.at[feat, where], sibling,
        )

    def diagonal_own(role):
        where = me if role == 0 else chips
        return pltpu.make_async_copy(
            grads.at[me, role, feat], terms_hbm.at[feat, where], keep_own_sem.at[chips - role * chips + role * me]
        )

    def term_arrival(kind, where):
        return remote(
            staged.at[0], terms_hbm.at[kind, where], keep_send_sem.at[0],
            term_recv_sem.at[kind, where], sibling,
        )

    def each_peer(action, sign):
        def body(window, _):
            for d in range(span):
                peer, core = window_step(window, d, sign)
                if d == 0:
                    pl.when(peer != me)(functools.partial(action, peer, core))
                else:
                    action(peer, core)
            return 0

        lax.fori_loop(0, span * span, body, 0)

    emb_copy = pltpu.make_async_copy(emb_hbm, emb, entry_sem.at[0])
    pairs_copy = pltpu.make_async_copy(pairs_hbm, pairs, entry_sem.at[1])
    counts_copy = pltpu.make_async_copy(counts_hbm, counts, entry_sem.at[2])
    pairs_copy.start()
    emb_copy.start()
    counts_copy.start()
    barrier = pltpu.get_barrier_semaphore()
    pl.semaphore_signal(barrier, 1, device_id=sibling, device_id_type=MESH)

    def greet(peer, core):
        for core in range(2):
            pl.semaphore_signal(barrier, 1, device_id=place(peer, core), device_id_type=MESH)

    each_peer(greet, 1)
    gains[feat] = gain_ref[...]
    pairs_copy.wait()
    emb_copy.wait()

    def stage(step, _):
        for j in range(4):
            peer = step * 4 + j
            staged[peer] = emb[sent_id(peer)]
        return 0

    lax.fori_loop(0, chips // 4, stage, 0)
    staged_sib[me] = emb[diagonal_id(other, 0)]
    staged[me] = emb[diagonal_id(other, 1)]

    pl.semaphore_wait(barrier, 2 * chips - 1)
    gain_scale = remote(
        gain_ref, gains.at[feat], small_send_sem.at[0], small_recv_sem.at[0], sibling
    )

    def send(peer, core):
        block_copy(peer, core).start()

        @pl.when(peer > me)
        def _():
            label_copy(peer, core).start()

    each_peer(send, 1)

    gain_scale.start()
    sib_copy(me).start()
    diagonal_col_copy().start()
    label_own(me, feat).start()
    blocks[me, 0, feat] = emb[diagonal_id(feat, 0)]
    blocks[me, 1, feat] = emb[diagonal_id(feat, 1)]

    def keep(peer, core):
        @pl.when(core == other)
        def _():
            staged_sib[peer] = emb[kept_id(peer)]
            sib_copy(peer).start()

        @pl.when(core == feat)
        def _():
            blocks[peer, kept_role(peer), feat] = emb[kept_id(peer)]

            @pl.when(peer > me)
            def _():
                label_own(peer, 0).start()

    each_peer(keep, -1)

    def list_ids(peer, _):
        on_diagonal = peer == me
        ids_out[0, peer] = jnp.where(on_diagonal, diagonal_id(0, 0), sent_id(peer))
        ids_out[1, peer] = jnp.where(on_diagonal, diagonal_id(1, 0), kept_id(peer))
        return 0

    lax.fori_loop(0, chips, list_ids, 0)
    for slot in range(2):
        ids_out[slot, chips] = diagonal_id(slot, 1)
    counts_copy.wait()

    def live(peer):
        at_requester = jnp.where(counts[me, peer] > 0, 1.0, 0.0)
        at_owner = jnp.where(counts[peer, me] > 1, 1.0, 0.0)
        worked = jnp.where(peer > me, at_requester, at_owner)
        return jnp.where(peer == me, 0.0, worked)

    gain_scale.wait_recv()
    gain_pair = jnp.concatenate([gains[feat], gains[other]], axis=-1)

    def tile(peer, goes_to, is_live, gain_sum):
        rows = jnp.concatenate([blocks[peer, 0, feat], blocks[peer, 0, other]], axis=-1)
        col = jnp.concatenate([blocks[peer, 1, feat], blocks[peer, 1, other]], axis=-1)
        rows_wide = rows.astype(jnp.float32)
        scaled = (rows_wide * gain_pair).astype(jnp.bfloat16)
        logits = lax.dot_general(
            scaled, col, (((1,), (1,)), ((), ())), preferred_element_type=jnp.float32
        )
        prob = 0.5 * jnp.tanh(0.5 * logits) + 0.5
        residual = ((prob - labels[peer].astype(jnp.float32)) * is_live).astype(jnp.bfloat16)
        pulled = jnp.dot(residual, col, preferred_element_type=jnp.float32)
        row_term = (pulled * gain_pair).astype(jnp.bfloat16)
        col_term = lax.dot_general(
            residual, scaled, (((0,), (0,)), ((), ())), preferred_element_type=jnp.float32
        ).astype(jnp.bfloat16)
        grads[goes_to, 0, feat] = row_term[:, :width]
        grads[goes_to, 0, other] = row_term[:, width:]
        grads[goes_to, 1, feat] = col_term[:, :width]
        grads[goes_to, 1, other] = col_term[:, width:]
        product = rows_wide * pulled
        return gain_sum + jnp.sum(product.reshape(-1, 8, 2 * width), axis=0)

    sib_arrival(me).wait_recv()
    diagonal_col_arrival().wait_recv()
    label_own(me, feat).wait()
    gain_sum = tile(
        me, me, jnp.where(counts[me, me] > feat, 1.0, 0.0), jnp.zeros((8, 2 * width), jnp.float32)
    )
    for role in range(2):
        diagonal_copy(role).start()
        diagonal_own(role).start()

    def mine(group, j):
        window = 2 * group + j // (span // 2)
        d = lax.rem(feat + window, 2) + 2 * (j % (span // 2))
        return window_step(window, d, -1)[0]

    def work(group, gain_sum):
        peers = [mine(group, j) for j in range(span)]
        for peer in peers:

            @pl.when(peer != me)
            def _(peer=peer):
                sib_arrival(peer).wait_recv()
                for half in range(2):
                    block_arrival(peer, half).wait_recv()

            @pl.when(peer > me)
            def _(peer=peer):
                label_own(peer, 0).wait()

            @pl.when(peer < me)
            def _(peer=peer):
                for half in range(2):
                    label_arrival(peer, half).wait_recv()

        for peer in peers:
            gain_sum = tile(peer, jnp.where(peer == me, chips, peer), live(peer), gain_sum)
        for peer in peers:

            @pl.when(peer != me)
            def _(peer=peer):
                for half in range(2):
                    back_copy(peer, half).start()
                keep_copy(peer).start()
                keep_own(peer).start()

        return gain_sum

    gain_sum = lax.fori_loop(0, chips // (2 * span), work, gain_sum)

    gain_sum = jnp.sum(gain_sum, axis=0, keepdims=True)
    gain_send[0] = gain_sum[:, width:]
    gain_pairwise = remote(
        gain_send.at[0], gain_sib, small_send_sem.at[1], small_recv_sem.at[1], sibling
    )
    gain_pairwise.start()
    gain_pairwise.wait_recv()
    chip_gain = gain_sum[:, :width] + gain_sib[...]
    gain_send[1] = chip_gain
    gain_all[me] = chip_gain

    def gain_copy(peer):
        return remote(
            gain_send.at[1], gain_all.at[me], gain_send_sem.at[peer],
            gain_recv_sem.at[me], place(peer, feat),
        )

    def gain_arrival(peer):
        return remote(
            gain_send.at[1], gain_all.at[peer], gain_send_sem.at[peer],
            gain_recv_sem.at[peer], sibling,
        )

    each_peer(lambda peer, core: gain_copy(peer).start(), 1)

    def drain(peer, core):
        block_copy(peer, core).wait_send()

        @pl.when(peer > me)
        def _():
            label_copy(peer, core).wait_send()

        term_arrival(0, peer).wait_recv()

        @pl.when(core == other)
        def _():
            sib_copy(peer).wait_send()
            term_arrival(1, peer).wait_recv()

        @pl.when(core == feat)
        def _():
            for half in range(2):
                back_copy(peer, half).wait_send()
            keep_copy(peer).wait_send()
            keep_own(peer).wait()

    each_peer(drain, 1)

    def wait_gain(peer, core):
        gain_arrival(peer).wait_recv()
        gain_copy(peer).wait_send()

    each_peer(wait_gain, 1)

    def add_gain(chip, total):
        return total + gain_all[chip]

    total = lax.fori_loop(0, chips, add_gain, jnp.zeros((1, width), jnp.float32))
    gain_out[...] = total * (16.0 / (chips * emb.shape[1]))

    for role in range(2):
        diagonal_copy(role).wait_send()
        diagonal_own(role).wait()
        term_arrival(other, me if role == 0 else chips).wait_recv()
    sib_copy(me).wait_send()
    diagonal_col_copy().wait_send()
    gain_scale.wait_send()
    gain_pairwise.wait_send()


def add_kernel(ids, terms_ref, gain_ref, out_ref, gain_out):
    gain_out[...] = gain_ref[...]
    out_ref[...] = jnp.zeros_like(out_ref)
    places = terms_ref.shape[1]

    def add(where, _):
        for slot in range(2):
            block = ids[slot, where]
            out_ref[block] += terms_ref[slot, where].astype(jnp.float32)
        return 0

    lax.fori_loop(0, places, add, 0)


def local(embeddings, decoder_gain, block_pairs, pair_counts, edge_labels):
    span = lax.axis_size("partner")
    chips = lax.axis_size("row") * span
    tile = edge_labels.shape[-1]
    width = embeddings.shape[1]
    count = embeddings.shape[0] // tile
    resident = embeddings.reshape(count, tile, width)
    labels = edge_labels.reshape(chips, 2, tile, tile)
    pairs = block_pairs.transpose(0, 2, 3, 1)

    smem = pl.BlockSpec(memory_space=pltpu.SMEM)
    vmem = pl.BlockSpec(memory_space=pltpu.VMEM)
    anywhere = pl.BlockSpec(memory_space=pl.ANY)
    dma = pltpu.SemaphoreType.DMA
    half = jnp.bfloat16
    terms, gain_total, ids = pl.pallas_call(
        functools.partial(exchange_kernel, chips, span),
        out_shape=(
            jax.ShapeDtypeStruct((2, chips + 1, tile, width), half),
            jax.ShapeDtypeStruct((1, width), jnp.float32),
            jax.ShapeDtypeStruct((2, chips + 1), jnp.int32),
        ),
        in_specs=[vmem, anywhere, anywhere, anywhere, anywhere],
        out_specs=(anywhere, vmem, smem),
        scratch_shapes=[
            pltpu.SMEM((chips, 2, 2, chips), jnp.int32),
            pltpu.SMEM((chips, chips), jnp.int32),
            pltpu.VMEM((count, tile, width), half),
            pltpu.VMEM((chips, tile, width), half),
            pltpu.VMEM((chips, tile, width), half),
            pltpu.VMEM((chips, 2, 2, tile, width), half),
            pltpu.VMEM((chips, tile, tile), half),
            pltpu.VMEM((chips + 1, 2, 2, tile, width), half),
            pltpu.VMEM((2, 1, width), jnp.float32),
            pltpu.VMEM((2, 1, width), jnp.float32),
            pltpu.VMEM((1, width), jnp.float32),
            pltpu.VMEM((chips, 1, width), jnp.float32),
            dma((3,)),
            dma((chips,)),
            dma((chips, 2)),
            dma((chips,)),
            dma((chips, 2)),
            dma((chips,)),
            dma((chips,)),
            dma((chips,)),
            dma((chips, 2)),
            dma((chips,)),
            dma((chips + 1,)),
            dma((2, chips + 1)),
            dma((2,)),
            dma((2,)),
            dma((chips,)),
            dma((chips,)),
        ],
        compiler_params=pltpu.CompilerParams(
            collective_id=0, has_side_effects=True, vmem_limit_bytes=56 * 2**20
        ),
        name="exchange",
    )(decoder_gain.reshape(1, width), pairs, pair_counts, resident, labels)

    part = tile // NODE_SPLIT
    grad, gain = pl.pallas_call(
        add_kernel,
        grid_spec=pltpu.PrefetchScalarGridSpec(
            num_scalar_prefetch=1,
            grid=(NODE_SPLIT,),
            in_specs=[
                pl.BlockSpec((2, chips + 1, part, width), lambda i, ids: (0, 0, i, 0)),
                pl.BlockSpec((1, width), lambda i, ids: (0, 0)),
            ],
            out_specs=(
                pl.BlockSpec((count, part, width), lambda i, ids: (0, i, 0)),
                pl.BlockSpec((1, width), lambda i, ids: (0, 0)),
            ),
        ),
        out_shape=(
            jax.ShapeDtypeStruct((count, tile, width), jnp.float32),
            jax.ShapeDtypeStruct((1, width), jnp.float32),
        ),
        compiler_params=pltpu.CompilerParams(vmem_limit_bytes=60 * 2**20),
        name="add_terms",
    )(ids, terms, gain_total)
    return grad.reshape(count * tile, width), gain.reshape(width)


def solution(mesh):
    in_specs = (
        P(("row", "partner"), "feat"),
        P("feat"),
        P(),
        P(),
        P(("row", "partner"), None, None, None, None),
    )
    out_specs = (P(("row", "partner"), "feat"), P("feat"))
    return jax.shard_map(local, mesh=mesh, in_specs=in_specs, out_specs=out_specs, check_vma=False)
```

```python
import functools

import jax
import jax.numpy as jnp
from jax import lax
from jax.experimental import pallas as pl
from jax.experimental.pallas import tpu as pltpu
from jax.sharding import PartitionSpec as P

NODE_SPLIT = 2
MESH = pl.DeviceIdType.MESH


def exchange_kernel(
    chips,
    span,
    gain_ref,
    pairs_hbm,
    counts_hbm,
    emb_hbm,
    labels_hbm,
    terms_hbm,
    gain_out,
    ids_out,
    pairs,
    counts,
    emb,
    staged,
    staged_sib,
    blocks,
    labels,
    grads,
    gains,
    gain_send,
    gain_sib,
    gain_all,
    entry_sem,
    arrive_sem,
    label_send_sem,
    send_sem,
    term_sem,
    small_sem,
):
    row = lax.axis_index("row")
    x, y, z = row // span, lax.axis_index("partner"), row % span
    me = row * span + y
    feat = lax.axis_index("feat")
    other = 1 - feat
    width = emb.shape[-1]
    half_rows = labels.shape[1] // 2
    my_rows = pl.ds(pl.multiple_of(feat * half_rows, half_rows), half_rows)

    def place(chip, core):
        return (chip // span, chip % span, core)

    sibling = place(me, other)

    def remote(src, dst, send, recv, where):
        return pltpu.make_async_remote_copy(
            src_ref=src, dst_ref=dst, send_sem=send, recv_sem=recv,
            device_id=where, device_id_type=MESH,
        )

    count = emb.shape[0]
    base = me * count

    def resident(block):
        return jnp.clip(block - base, 0, count - 1)

    def sent_id(peer):
        return resident(jnp.where(peer > me, pairs[me, 1, 0, peer], pairs[peer, 0, 1, me]))

    def kept_id(peer):
        return resident(jnp.where(peer > me, pairs[me, 0, 0, peer], pairs[peer, 1, 1, me]))

    def diagonal_id(slot, role):
        return resident(pairs[me, slot, role, me])

    def window_step(window, d, sign):
        b, c = lax.rem(window, span), lax.div(window, span)
        dx, dy = lax.rem(d + b, span), lax.rem(d + c, span)
        if sign < 0:
            dx, dy, d = span - dx, span - dy, span - d
        px, py, pz = lax.rem(x + dx, span), lax.rem(y + dy, span), lax.rem(z + d, span)
        return (px * span + pz) * span + py, lax.rem(dx, 2)

    groups = chips // (2 * span)
    block_sends, sib_sends, back_sends, diagonal_sends, gain_sends = (
        send_sem.at[k] for k in range(5)
    )

    def wait_bytes(ref, sem):
        pltpu.make_async_copy(ref, ref, sem).wait()

    def group_of(window):
        return arrive_sem.at[lax.div(window, 2)]

    def kept_role(peer):
        return jnp.where(peer < me, 1, 0)

    def block_copy(peer, core, window):
        role = jnp.where(peer > me, 0, 1)
        return remote(
            staged.at[peer], blocks.at[me, role, feat], block_sends, group_of(window),
            place(peer, core),
        )

    def label_copy(peer, core, window):
        return remote(
            labels_hbm.at[peer, 1, my_rows], labels.at[me, my_rows], label_send_sem.at[peer],
            group_of(window), place(peer, core),
        )

    def label_own(peer, slot, sem):
        return pltpu.make_async_copy(labels_hbm.at[peer, slot], labels.at[peer], sem)

    def sib_copy(peer, sem):
        return remote(
            staged_sib.at[peer], blocks.at[peer, kept_role(peer), feat], sib_sends, sem, sibling
        )

    def diagonal_col_copy():
        return remote(
            staged.at[me], blocks.at[me, 1, feat], block_sends, arrive_sem.at[groups], sibling
        )

    def back_copy(peer, half):
        return remote(
            grads.at[peer, 1 - kept_role(peer), half], terms_hbm.at[0, me], back_sends,
            term_sem.at[0], place(peer, half),
        )

    def keep_copy(peer):
        return remote(
            grads.at[peer, kept_role(peer), other], terms_hbm.at[1, peer], sib_sends,
            term_sem.at[1], sibling,
        )

    def keep_own(peer):
        return pltpu.make_async_copy(
            grads.at[peer, kept_role(peer), feat], terms_hbm.at[1, peer], term_sem.at[1]
        )

    def diagonal_copy(role):
        where = me if role == 0 else chips
        return remote(
            grads.at[me, role, other], terms_hbm.at[feat, where], diagonal_sends,
            term_sem.at[0], sibling,
        )

    def diagonal_own(role):
        where = me if role == 0 else chips
        return pltpu.make_async_copy(
            grads.at[me, role, feat], terms_hbm.at[feat, where], term_sem.at[1]
        )

    def each_peer(action, sign):
        def body(window, _):
            for d in range(span):
                peer, core = window_step(window, d, sign)
                if d == 0:
                    pl.when(peer != me)(functools.partial(action, peer, core, window))
                else:
                    action(peer, core, window)
            return 0

        lax.fori_loop(0, span * span, body, 0)

    emb_copy = pltpu.make_async_copy(emb_hbm, emb, entry_sem.at[0])
    pairs_copy = pltpu.make_async_copy(pairs_hbm, pairs, entry_sem.at[1])
    counts_copy = pltpu.make_async_copy(counts_hbm, counts, entry_sem.at[2])
    pairs_copy.start()
    emb_copy.start()
    counts_copy.start()
    barrier = pltpu.get_barrier_semaphore()
    pl.semaphore_signal(barrier, 1, device_id=sibling, device_id_type=MESH)

    def greet(peer, core, window):
        for core in range(2):
            pl.semaphore_signal(barrier, 1, device_id=place(peer, core), device_id_type=MESH)

    each_peer(greet, 1)
    gains[feat] = gain_ref[...]
    pairs_copy.wait()
    emb_copy.wait()

    def stage(step, _):
        for j in range(4):
            peer = step * 4 + j
            staged[peer] = emb[sent_id(peer)]
        return 0

    lax.fori_loop(0, chips // 4, stage, 0)
    staged_sib[me] = emb[diagonal_id(other, 0)]
    staged[me] = emb[diagonal_id(other, 1)]

    pl.semaphore_wait(barrier, 2 * chips - 1)
    gain_scale = remote(
        gain_ref, gains.at[feat], small_sem.at[0], small_sem.at[1], sibling
    )

    def send(peer, core, window):
        block_copy(peer, core, window).start()

        @pl.when(peer > me)
        def _():
            label_copy(peer, core, window).start()

    each_peer(send, 1)

    gain_scale.start()
    sib_copy(me, arrive_sem.at[groups]).start()
    diagonal_col_copy().start()
    label_own(me, feat, arrive_sem.at[groups]).start()
    blocks[me, 0, feat] = emb[diagonal_id(feat, 0)]
    blocks[me, 1, feat] = emb[diagonal_id(feat, 1)]

    def keep(peer, core, window):
        @pl.when(core == other)
        def _():
            staged_sib[peer] = emb[kept_id(peer)]
            sib_copy(peer, group_of(window)).start()

        @pl.when(core == feat)
        def _():
            blocks[peer, kept_role(peer), feat] = emb[kept_id(peer)]

            @pl.when(peer > me)
            def _():
                label_own(peer, 0, group_of(window)).start()

    each_peer(keep, -1)

    def list_ids(peer, _):
        on_diagonal = peer == me
        ids_out[0, peer] = jnp.where(on_diagonal, diagonal_id(0, 0), sent_id(peer))
        ids_out[1, peer] = jnp.where(on_diagonal, diagonal_id(1, 0), kept_id(peer))
        return 0

    lax.fori_loop(0, chips, list_ids, 0)
    for slot in range(2):
        ids_out[slot, chips] = diagonal_id(slot, 1)
    counts_copy.wait()

    def live(peer):
        at_requester = jnp.where(counts[me, peer] > 0, 1.0, 0.0)
        at_owner = jnp.where(counts[peer, me] > 1, 1.0, 0.0)
        worked = jnp.where(peer > me, at_requester, at_owner)
        return jnp.where(peer == me, 0.0, worked)

    gain_scale.wait_recv()
    gain_pair = jnp.concatenate([gains[feat], gains[other]], axis=-1)

    def tile(peer, goes_to, is_live, gain_sum):
        rows = jnp.concatenate([blocks[peer, 0, feat], blocks[peer, 0, other]], axis=-1)
        col = jnp.concatenate([blocks[peer, 1, feat], blocks[peer, 1, other]], axis=-1)
        rows_wide = rows.astype(jnp.float32)
        scaled = (rows_wide * gain_pair).astype(jnp.bfloat16)
        logits = lax.dot_general(
            scaled, col, (((1,), (1,)), ((), ())), preferred_element_type=jnp.float32
        )
        prob = 0.5 * jnp.tanh(0.5 * logits) + 0.5
        residual = ((prob - labels[peer].astype(jnp.float32)) * is_live).astype(jnp.bfloat16)
        pulled = jnp.dot(residual, col, preferred_element_type=jnp.float32)
        row_term = (pulled * gain_pair).astype(jnp.bfloat16)
        col_term = lax.dot_general(
            residual, scaled, (((0,), (0,)), ((), ())), preferred_element_type=jnp.float32
        ).astype(jnp.bfloat16)
        grads[goes_to, 0, feat] = row_term[:, :width]
        grads[goes_to, 0, other] = row_term[:, width:]
        grads[goes_to, 1, feat] = col_term[:, :width]
        grads[goes_to, 1, other] = col_term[:, width:]
        product = rows_wide * pulled
        return gain_sum + jnp.sum(product.reshape(-1, 8, 2 * width), axis=0)

    wait_bytes(staged.at[pl.ds(0, 3)], arrive_sem.at[groups])
    gain_sum = tile(
        me, me, jnp.where(counts[me, me] > feat, 1.0, 0.0), jnp.zeros((8, 2 * width), jnp.float32)
    )
    for role in range(2):
        diagonal_copy(role).start()
        diagonal_own(role).start()

    def mine(group, j):
        window = 2 * group + j // (span // 2)
        d = lax.rem(feat + window, 2) + 2 * (j % (span // 2))
        return window_step(window, d, -1)[0]

    def work(group, gain_sum):
        peers = [mine(group, j) for j in range(span)]
        short = (group == 0) & (feat == 0)

        @pl.when(short)
        def _():
            wait_bytes(blocks.at[pl.ds(0, span - 1)], arrive_sem.at[0])

        @pl.when(jnp.logical_not(short))
        def _():
            wait_bytes(blocks.at[pl.ds(0, span)], arrive_sem.at[group])

        for peer in peers:
            gain_sum = tile(peer, jnp.where(peer == me, chips, peer), live(peer), gain_sum)
        for peer in peers:

            @pl.when(peer != me)
            def _(peer=peer):
                for half in range(2):
                    back_copy(peer, half).start()
                keep_copy(peer).start()
                keep_own(peer).start()

        return gain_sum

    gain_sum = lax.fori_loop(0, groups, work, gain_sum)

    gain_sum = jnp.sum(gain_sum, axis=0, keepdims=True)
    gain_send[0] = gain_sum[:, width:]
    gain_pairwise = remote(
        gain_send.at[0], gain_sib, small_sem.at[2], small_sem.at[3], sibling
    )
    gain_pairwise.start()
    gain_pairwise.wait_recv()
    chip_gain = gain_sum[:, :width] + gain_sib[...]
    gain_send[1] = chip_gain
    gain_all[me] = chip_gain

    def start_gain(peer, core, window):
        remote(
            gain_send.at[1], gain_all.at[me], gain_sends, small_sem.at[4], place(peer, feat)
        ).start()

    each_peer(start_gain, 1)

    wait_bytes(terms_hbm.at[1], term_sem.at[1])
    wait_bytes(staged, block_sends)
    wait_bytes(staged, sib_sends)
    wait_bytes(grads.at[0, 0], diagonal_sends)
    half_peers = chips // 2

    @pl.when(feat == 0)
    def _():
        wait_bytes(grads.at[pl.ds(0, half_peers - 1), 0], back_sends)

    @pl.when(feat == 1)
    def _():
        wait_bytes(grads.at[pl.ds(0, half_peers), 0], back_sends)

    def drain_label(peer, core, window):
        @pl.when(peer > me)
        def _():
            label_copy(peer, core, window).wait_send()

    each_peer(drain_label, 1)
    wait_bytes(gain_all.at[pl.ds(0, chips - 1)], gain_sends)
    wait_bytes(gain_all.at[pl.ds(0, chips - 1)], small_sem.at[4])

    def add_gain(chip, total):
        return total + gain_all[chip]

    total = lax.fori_loop(0, chips, add_gain, jnp.zeros((1, width), jnp.float32))
    gain_out[...] = total * (16.0 / (chips * emb.shape[1]))

    wait_bytes(terms_hbm.at[0], term_sem.at[0])
    gain_scale.wait_send()
    gain_pairwise.wait_send()


def add_kernel(ids, terms_ref, gain_ref, out_ref, gain_out):
    gain_out[...] = gain_ref[...]
    out_ref[...] = jnp.zeros_like(out_ref)
    places = terms_ref.shape[1]

    def add(where, _):
        for slot in range(2):
            block = ids[slot, where]
            out_ref[block] += terms_ref[slot, where].astype(jnp.float32)
        return 0

    lax.fori_loop(0, places, add, 0)


def local(embeddings, decoder_gain, block_pairs, pair_counts, edge_labels):
    span = lax.axis_size("partner")
    chips = lax.axis_size("row") * span
    tile = edge_labels.shape[-1]
    width = embeddings.shape[1]
    count = embeddings.shape[0] // tile
    resident = embeddings.reshape(count, tile, width)
    labels = edge_labels.reshape(chips, 2, tile, tile)
    pairs = block_pairs.transpose(0, 2, 3, 1)

    smem = pl.BlockSpec(memory_space=pltpu.SMEM)
    vmem = pl.BlockSpec(memory_space=pltpu.VMEM)
    anywhere = pl.BlockSpec(memory_space=pl.ANY)
    dma = pltpu.SemaphoreType.DMA
    half = jnp.bfloat16
    terms, gain_total, ids = pl.pallas_call(
        functools.partial(exchange_kernel, chips, span),
        out_shape=(
            jax.ShapeDtypeStruct((2, chips + 1, tile, width), half),
            jax.ShapeDtypeStruct((1, width), jnp.float32),
            jax.ShapeDtypeStruct((2, chips + 1), jnp.int32),
        ),
        in_specs=[vmem, anywhere, anywhere, anywhere, anywhere],
        out_specs=(anywhere, vmem, smem),
        scratch_shapes=[
            pltpu.SMEM((chips, 2, 2, chips), jnp.int32),
            pltpu.SMEM((chips, chips), jnp.int32),
            pltpu.VMEM((count, tile, width), half),
            pltpu.VMEM((chips, tile, width), half),
            pltpu.VMEM((chips, tile, width), half),
            pltpu.VMEM((chips, 2, 2, tile, width), half),
            pltpu.VMEM((chips, tile, tile), half),
            pltpu.VMEM((chips + 1, 2, 2, tile, width), half),
            pltpu.VMEM((2, 1, width), jnp.float32),
            pltpu.VMEM((2, 1, width), jnp.float32),
            pltpu.VMEM((1, width), jnp.float32),
            pltpu.VMEM((chips, 1, width), jnp.float32),
            dma((3,)),
            dma((chips // (2 * span) + 1,)),
            dma((chips,)),
            dma((5,)),
            dma((2,)),
            dma((5,)),
        ],
        compiler_params=pltpu.CompilerParams(
            collective_id=0, has_side_effects=True, vmem_limit_bytes=56 * 2**20
        ),
        name="exchange",
    )(decoder_gain.reshape(1, width), pairs, pair_counts, resident, labels)

    part = tile // NODE_SPLIT
    grad, gain = pl.pallas_call(
        add_kernel,
        grid_spec=pltpu.PrefetchScalarGridSpec(
            num_scalar_prefetch=1,
            grid=(NODE_SPLIT,),
            in_specs=[
                pl.BlockSpec((2, chips + 1, part, width), lambda i, ids: (0, 0, i, 0)),
                pl.BlockSpec((1, width), lambda i, ids: (0, 0)),
            ],
            out_specs=(
                pl.BlockSpec((count, part, width), lambda i, ids: (0, i, 0)),
                pl.BlockSpec((1, width), lambda i, ids: (0, 0)),
            ),
        ),
        out_shape=(
            jax.ShapeDtypeStruct((count, tile, width), jnp.float32),
            jax.ShapeDtypeStruct((1, width), jnp.float32),
        ),
        compiler_params=pltpu.CompilerParams(vmem_limit_bytes=60 * 2**20),
        name="add_terms",
    )(ids, terms, gain_total)
    return grad.reshape(count * tile, width), gain.reshape(width)


def solution(mesh):
    in_specs = (
        P(("row", "partner"), "feat"),
        P("feat"),
        P(),
        P(),
        P(("row", "partner"), None, None, None, None),
    )
    out_specs = (P(("row", "partner"), "feat"), P("feat"))
    return jax.shard_map(local, mesh=mesh, in_specs=in_specs, out_specs=out_specs, check_vma=False)
```

```python
import functools

import jax
import jax.numpy as jnp
from jax import lax
from jax.experimental import pallas as pl
from jax.experimental.pallas import tpu as pltpu
from jax.sharding import PartitionSpec as P

PIECES = 8
MESH = pl.DeviceIdType.MESH


def exchange_kernel(
    chips,
    span,
    gain_ref,
    pairs_hbm,
    counts_hbm,
    emb_hbm,
    labels_hbm,
    terms,
    gain_out,
    ids_out,
    pairs,
    counts,
    emb,
    staged,
    staged_sib,
    blocks,
    labels,
    grads,
    gains,
    gain_send,
    gain_sib,
    gain_all,
    entry_sem,
    arrive_sem,
    label_send_sem,
    send_sem,
    term_sem,
    small_sem,
):
    row = lax.axis_index("row")
    x, y, z = row // span, lax.axis_index("partner"), row % span
    me = row * span + y
    feat = lax.axis_index("feat")
    other = 1 - feat
    width = emb.shape[-1]
    half_rows = labels.shape[1] // 2
    my_rows = pl.ds(pl.multiple_of(feat * half_rows, half_rows), half_rows)

    def place(chip, core):
        return (chip // span, chip % span, core)

    sibling = place(me, other)

    def remote(src, dst, send, recv, where):
        return pltpu.make_async_remote_copy(
            src_ref=src, dst_ref=dst, send_sem=send, recv_sem=recv,
            device_id=where, device_id_type=MESH,
        )

    count = emb.shape[0]
    base = me * count

    def resident(block):
        return jnp.clip(block - base, 0, count - 1)

    def sent_id(peer):
        return resident(jnp.where(peer > me, pairs[me, 1, 0, peer], pairs[peer, 0, 1, me]))

    def kept_id(peer):
        return resident(jnp.where(peer > me, pairs[me, 0, 0, peer], pairs[peer, 1, 1, me]))

    def diagonal_id(slot, role):
        return resident(pairs[me, slot, role, me])

    def window_step(window, d, sign):
        b, c = lax.rem(window, span), lax.div(window, span)
        dx, dy = lax.rem(d + b, span), lax.rem(d + c, span)
        if sign < 0:
            dx, dy, d = span - dx, span - dy, span - d
        px, py, pz = lax.rem(x + dx, span), lax.rem(y + dy, span), lax.rem(z + d, span)
        return (px * span + pz) * span + py, lax.rem(dx, 2)

    groups = chips // (2 * span)
    places = chips + 1
    block_sends, sib_sends, back_sends, diagonal_sends, gain_sends = (
        send_sem.at[k] for k in range(5)
    )

    def wait_bytes(ref, sem):
        pltpu.make_async_copy(ref, ref, sem).wait()

    def group_of(window):
        return arrive_sem.at[lax.div(window, 2)]

    def kept_role(peer):
        return jnp.where(peer < me, 1, 0)

    def block_copy(peer, core, window):
        role = jnp.where(peer > me, 0, 1)
        return remote(
            staged.at[peer], blocks.at[me, role, feat], block_sends, group_of(window),
            place(peer, core),
        )

    def label_copy(peer, core, window):
        return remote(
            labels_hbm.at[peer, 1, my_rows], labels.at[me, my_rows], label_send_sem.at[peer],
            group_of(window), place(peer, core),
        )

    def label_own(peer, slot, sem):
        return pltpu.make_async_copy(labels_hbm.at[peer, slot], labels.at[peer], sem)

    def sib_copy(peer, sem):
        return remote(
            staged_sib.at[peer], blocks.at[peer, kept_role(peer), feat], sib_sends, sem, sibling
        )

    def diagonal_col_copy():
        return remote(
            staged.at[me], blocks.at[me, 1, feat], block_sends, arrive_sem.at[groups], sibling
        )

    def back_copy(peer, half):
        return remote(
            grads.at[peer, 1 - kept_role(peer), half], terms.at[me], back_sends,
            term_sem.at[0], place(peer, half),
        )

    def keep_copy(peer):
        return remote(
            grads.at[peer, kept_role(peer), other], terms.at[places + peer], sib_sends,
            term_sem.at[1], sibling,
        )

    def keep_own(peer):
        return pltpu.make_async_copy(
            grads.at[peer, kept_role(peer), feat], terms.at[places + peer], term_sem.at[1]
        )

    def diagonal_copy(role):
        where = me if role == 0 else chips
        return remote(
            grads.at[me, role, other], terms.at[feat * places + where], diagonal_sends,
            term_sem.at[0], sibling,
        )

    def diagonal_own(role):
        where = me if role == 0 else chips
        return pltpu.make_async_copy(
            grads.at[me, role, feat], terms.at[feat * places + where], term_sem.at[1]
        )

    def each_peer(action, sign):
        def body(window, _):
            for d in range(span):
                peer, core = window_step(window, d, sign)
                if d == 0:
                    pl.when(peer != me)(functools.partial(action, peer, core, window))
                else:
                    action(peer, core, window)
            return 0

        lax.fori_loop(0, span * span, body, 0)

    emb_copy = pltpu.make_async_copy(emb_hbm, emb, entry_sem.at[0])
    pairs_copy = pltpu.make_async_copy(pairs_hbm, pairs, entry_sem.at[1])
    counts_copy = pltpu.make_async_copy(counts_hbm, counts, entry_sem.at[2])
    pairs_copy.start()
    emb_copy.start()
    counts_copy.start()
    barrier = pltpu.get_barrier_semaphore()
    pl.semaphore_signal(barrier, 1, device_id=sibling, device_id_type=MESH)

    def greet(peer, core, window):
        for core in range(2):
            pl.semaphore_signal(barrier, 1, device_id=place(peer, core), device_id_type=MESH)

    each_peer(greet, 1)
    gains[feat] = gain_ref[...]
    pairs_copy.wait()
    emb_copy.wait()

    def stage(step, _):
        for j in range(4):
            peer = step * 4 + j
            staged[peer] = emb[sent_id(peer)]
        return 0

    lax.fori_loop(0, chips // 4, stage, 0)
    staged_sib[me] = emb[diagonal_id(other, 0)]
    staged[me] = emb[diagonal_id(other, 1)]

    pl.semaphore_wait(barrier, 2 * chips - 1)
    gain_scale = remote(
        gain_ref, gains.at[feat], small_sem.at[0], small_sem.at[1], sibling
    )

    def send(peer, core, window):
        block_copy(peer, core, window).start()

        @pl.when(peer > me)
        def _():
            label_copy(peer, core, window).start()

    each_peer(send, 1)

    gain_scale.start()
    sib_copy(me, arrive_sem.at[groups]).start()
    diagonal_col_copy().start()
    label_own(me, feat, arrive_sem.at[groups]).start()
    blocks[me, 0, feat] = emb[diagonal_id(feat, 0)]
    blocks[me, 1, feat] = emb[diagonal_id(feat, 1)]

    def keep(peer, core, window):
        @pl.when(core == other)
        def _():
            staged_sib[peer] = emb[kept_id(peer)]
            sib_copy(peer, group_of(window)).start()

        @pl.when(core == feat)
        def _():
            blocks[peer, kept_role(peer), feat] = emb[kept_id(peer)]

            @pl.when(peer > me)
            def _():
                label_own(peer, 0, group_of(window)).start()

    each_peer(keep, -1)

    def list_ids(peer, _):
        on_diagonal = peer == me
        ids_out[0, peer] = jnp.where(on_diagonal, diagonal_id(0, 0), sent_id(peer))
        ids_out[1, peer] = jnp.where(on_diagonal, diagonal_id(1, 0), kept_id(peer))
        return 0

    lax.fori_loop(0, chips, list_ids, 0)
    for slot in range(2):
        ids_out[slot, chips] = diagonal_id(slot, 1)
    counts_copy.wait()

    def live(peer):
        at_requester = jnp.where(counts[me, peer] > 0, 1.0, 0.0)
        at_owner = jnp.where(counts[peer, me] > 1, 1.0, 0.0)
        worked = jnp.where(peer > me, at_requester, at_owner)
        return jnp.where(peer == me, 0.0, worked)

    gain_scale.wait_recv()
    gain_pair = jnp.concatenate([gains[feat], gains[other]], axis=-1)

    def tile(peer, goes_to, is_live, gain_sum):
        rows = jnp.concatenate([blocks[peer, 0, feat], blocks[peer, 0, other]], axis=-1)
        col = jnp.concatenate([blocks[peer, 1, feat], blocks[peer, 1, other]], axis=-1)
        rows_wide = rows.astype(jnp.float32)
        scaled = (rows_wide * gain_pair).astype(jnp.bfloat16)
        logits = lax.dot_general(
            scaled, col, (((1,), (1,)), ((), ())), preferred_element_type=jnp.float32
        )
        prob = 0.5 * jnp.tanh(0.5 * logits) + 0.5
        residual = ((prob - labels[peer].astype(jnp.float32)) * is_live).astype(jnp.bfloat16)
        pulled = jnp.dot(residual, col, preferred_element_type=jnp.float32)
        row_term = (pulled * gain_pair).astype(jnp.bfloat16)
        col_term = lax.dot_general(
            residual, scaled, (((0,), (0,)), ((), ())), preferred_element_type=jnp.float32
        ).astype(jnp.bfloat16)
        grads[goes_to, 0, feat] = row_term[:, :width]
        grads[goes_to, 0, other] = row_term[:, width:]
        grads[goes_to, 1, feat] = col_term[:, :width]
        grads[goes_to, 1, other] = col_term[:, width:]
        product = rows_wide * pulled
        return gain_sum + jnp.sum(product.reshape(-1, 8, 2 * width), axis=0)

    wait_bytes(staged.at[pl.ds(0, 3)], arrive_sem.at[groups])
    gain_sum = tile(
        me, me, jnp.where(counts[me, me] > feat, 1.0, 0.0), jnp.zeros((8, 2 * width), jnp.float32)
    )
    for role in range(2):
        diagonal_copy(role).start()
        diagonal_own(role).start()

    def mine(group, j):
        window = 2 * group + j // (span // 2)
        d = lax.rem(feat + window, 2) + 2 * (j % (span // 2))
        return window_step(window, d, -1)[0]

    def work(group, gain_sum):
        peers = [mine(group, j) for j in range(span)]
        short = (group == 0) & (feat == 0)

        @pl.when(short)
        def _():
            wait_bytes(blocks.at[pl.ds(0, span - 1)], arrive_sem.at[0])

        @pl.when(jnp.logical_not(short))
        def _():
            wait_bytes(blocks.at[pl.ds(0, span)], arrive_sem.at[group])

        for peer in peers:
            gain_sum = tile(peer, jnp.where(peer == me, chips, peer), live(peer), gain_sum)
        for peer in peers:

            @pl.when(peer != me)
            def _(peer=peer):
                for half in range(2):
                    back_copy(peer, half).start()
                keep_copy(peer).start()
                keep_own(peer).start()

        return gain_sum

    gain_sum = lax.fori_loop(0, groups, work, gain_sum)

    gain_sum = jnp.sum(gain_sum, axis=0, keepdims=True)
    gain_send[0] = gain_sum[:, width:]
    gain_pairwise = remote(
        gain_send.at[0], gain_sib, small_sem.at[2], small_sem.at[3], sibling
    )
    gain_pairwise.start()
    gain_pairwise.wait_recv()
    chip_gain = gain_sum[:, :width] + gain_sib[...]
    gain_send[1] = chip_gain
    gain_all[me] = chip_gain

    def start_gain(peer, core, window):
        remote(
            gain_send.at[1], gain_all.at[me], gain_sends, small_sem.at[4], place(peer, feat)
        ).start()

    each_peer(start_gain, 1)

    wait_bytes(terms.at[pl.ds(places, places)], term_sem.at[1])
    wait_bytes(staged, block_sends)
    wait_bytes(staged, sib_sends)
    wait_bytes(grads.at[0, 0], diagonal_sends)
    half_peers = chips // 2

    @pl.when(feat == 0)
    def _():
        wait_bytes(grads.at[pl.ds(0, half_peers - 1), 0], back_sends)

    @pl.when(feat == 1)
    def _():
        wait_bytes(grads.at[pl.ds(0, half_peers), 0], back_sends)

    def drain_label(peer, core, window):
        @pl.when(peer > me)
        def _():
            label_copy(peer, core, window).wait_send()

    each_peer(drain_label, 1)
    wait_bytes(gain_all.at[pl.ds(0, chips - 1)], gain_sends)
    wait_bytes(gain_all.at[pl.ds(0, chips - 1)], small_sem.at[4])

    def add_gain(chip, total):
        return total + gain_all[chip]

    total = lax.fori_loop(0, chips, add_gain, jnp.zeros((1, width), jnp.float32))
    gain_out[...] = total * (16.0 / (chips * emb.shape[1]))

    wait_bytes(terms.at[pl.ds(0, places)], term_sem.at[0])
    gain_scale.wait_send()
    gain_pairwise.wait_send()


def add_kernel(ids, terms, gain_ref, out_hbm, gain_out, sums, head, following, out_sem):
    none = terms.shape[0]
    places = none // 2
    count = sums.shape[0]
    piece = count // PIECES

    def copy_out(k):
        span = pl.ds(k * piece, piece)
        return pltpu.make_async_copy(sums.at[span], out_hbm.at[span], out_sem.at[k])

    gain_out[...] = gain_ref[...]
    following[none] = none

    def clear(step, _):
        for j in range(4):
            head[step * 4 + j] = none
        return 0

    lax.fori_loop(0, count // 4, clear, 0)

    def link(place, _):
        for slot in range(2):
            term = slot * places + place
            block = ids[slot, place]
            following[term] = head[block]
            head[block] = term
        return 0

    lax.fori_loop(0, places, link, 0)

    def term_or_zero(t):
        return jnp.where(t < none, terms[jnp.minimum(t, none - 1)].astype(jnp.float32), 0.0)

    def four(step, _):
        blocks = [step * 4 + j for j in range(4)]
        first = [head[b] for b in blocks]
        second = [following[t] for t in first]
        third = [following[t] for t in second]
        for b, t, u in zip(blocks, first, second):
            sums[b] = term_or_zero(t) + term_or_zero(u)
        least = jnp.minimum(jnp.minimum(third[0], third[1]), jnp.minimum(third[2], third[3]))

        @pl.when(least < none)
        def _():
            for b, t in zip(blocks, third):

                def rest(t, b=b):
                    sums[b] += terms[t].astype(jnp.float32)
                    return following[t]

                lax.while_loop(lambda t: t < none, rest, t)

        return 0

    def one_piece(k, _):
        lax.fori_loop(k * (piece // 4), (k + 1) * (piece // 4), four, 0)
        copy_out(k).start()
        return 0

    lax.fori_loop(0, PIECES, one_piece, 0)

    def finish(k, _):
        copy_out(k).wait()
        return 0

    lax.fori_loop(0, PIECES, finish, 0)


def local(embeddings, decoder_gain, block_pairs, pair_counts, edge_labels):
    span = lax.axis_size("partner")
    chips = lax.axis_size("row") * span
    tile = edge_labels.shape[-1]
    width = embeddings.shape[1]
    count = embeddings.shape[0] // tile
    resident = embeddings.reshape(count, tile, width)
    labels = edge_labels.reshape(chips, 2, tile, tile)
    pairs = block_pairs.transpose(0, 2, 3, 1)

    smem = pl.BlockSpec(memory_space=pltpu.SMEM)
    vmem = pl.BlockSpec(memory_space=pltpu.VMEM)
    anywhere = pl.BlockSpec(memory_space=pl.ANY)
    dma = pltpu.SemaphoreType.DMA
    half = jnp.bfloat16
    terms, gain_total, ids = pl.pallas_call(
        functools.partial(exchange_kernel, chips, span),
        out_shape=(
            pltpu.VMEM((2 * (chips + 1), tile, width), half),
            pltpu.VMEM((1, width), jnp.float32),
            pltpu.SMEM((2, chips + 1), jnp.int32),
        ),
        in_specs=[vmem, anywhere, anywhere, anywhere, anywhere],
        out_specs=(vmem, vmem, smem),
        scratch_shapes=[
            pltpu.SMEM((chips, 2, 2, chips), jnp.int32),
            pltpu.SMEM((chips, chips), jnp.int32),
            pltpu.VMEM((count, tile, width), half),
            pltpu.VMEM((chips, tile, width), half),
            pltpu.VMEM((chips, tile, width), half),
            pltpu.VMEM((chips, 2, 2, tile, width), half),
            pltpu.VMEM((chips, tile, tile), half),
            pltpu.VMEM((chips + 1, 2, 2, tile, width), half),
            pltpu.VMEM((2, 1, width), jnp.float32),
            pltpu.VMEM((2, 1, width), jnp.float32),
            pltpu.VMEM((1, width), jnp.float32),
            pltpu.VMEM((chips, 1, width), jnp.float32),
            dma((3,)),
            dma((chips // (2 * span) + 1,)),
            dma((chips,)),
            dma((5,)),
            dma((2,)),
            dma((5,)),
        ],
        compiler_params=pltpu.CompilerParams(
            collective_id=0, has_side_effects=True, vmem_limit_bytes=56 * 2**20
        ),
        name="exchange",
    )(
        decoder_gain.reshape(1, width),
        *(
            pltpu.with_memory_space_constraint(array, pltpu.HBM)
            for array in (pairs, pair_counts, resident, labels)
        ),
    )

    places = 2 * (chips + 1)
    grad, gain = pl.pallas_call(
        add_kernel,
        in_specs=[smem, vmem, vmem],
        out_specs=(anywhere, vmem),
        out_shape=(
            jax.ShapeDtypeStruct((count, tile, width), jnp.float32),
            jax.ShapeDtypeStruct((1, width), jnp.float32),
        ),
        scratch_shapes=[
            pltpu.VMEM((count, tile, width), jnp.float32),
            pltpu.SMEM((count,), jnp.int32),
            pltpu.SMEM((places + 1,), jnp.int32),
            dma((PIECES,)),
        ],
        compiler_params=pltpu.CompilerParams(vmem_limit_bytes=48 * 2**20),
        name="add_terms",
    )(
        pltpu.with_memory_space_constraint(ids, pltpu.SMEM),
        pltpu.with_memory_space_constraint(terms, pltpu.VMEM),
        pltpu.with_memory_space_constraint(gain_total, pltpu.VMEM),
    )
    return grad.reshape(count * tile, width), gain.reshape(width)


def solution(mesh):
    in_specs = (
        P(("row", "partner"), "feat"),
        P("feat"),
        P(),
        P(),
        P(("row", "partner"), None, None, None, None),
    )
    out_specs = (P(("row", "partner"), "feat"), P("feat"))
    return jax.shard_map(local, mesh=mesh, in_specs=in_specs, out_specs=out_specs, check_vma=False)
```

```python
import functools

import jax
import jax.numpy as jnp
from jax import lax
from jax.experimental import pallas as pl
from jax.experimental.pallas import tpu as pltpu
from jax.sharding import PartitionSpec as P

PIECES = 8
MESH = pl.DeviceIdType.MESH


def exchange_kernel(
    chips,
    span,
    gain_ref,
    pairs_hbm,
    counts_hbm,
    emb_hbm,
    labels_hbm,
    terms,
    gain_out,
    ids_out,
    pairs,
    counts,
    emb,
    staged,
    staged_sib,
    blocks,
    labels,
    grads,
    gains,
    gain_send,
    gain_sib,
    gain_all,
    entry_sem,
    arrive_sem,
    label_send_sem,
    send_sem,
    term_sem,
    small_sem,
):
    row = lax.axis_index("row")
    x, y, z = row // span, lax.axis_index("partner"), row % span
    me = row * span + y
    feat = lax.axis_index("feat")
    other = 1 - feat
    width = emb.shape[-1]
    half_rows = labels.shape[1] // 2
    my_rows = pl.ds(pl.multiple_of(feat * half_rows, half_rows), half_rows)

    def place(chip, core):
        return (chip // span, chip % span, core)

    sibling = place(me, other)

    def remote(src, dst, send, recv, where):
        return pltpu.make_async_remote_copy(
            src_ref=src, dst_ref=dst, send_sem=send, recv_sem=recv,
            device_id=where, device_id_type=MESH,
        )

    count = emb.shape[0]
    base = me * count

    def resident(block):
        return jnp.clip(block - base, 0, count - 1)

    def sent_id(peer):
        return resident(jnp.where(peer > me, pairs[me, 1, 0, peer], pairs[peer, 0, 1, me]))

    def kept_id(peer):
        return resident(jnp.where(peer > me, pairs[me, 0, 0, peer], pairs[peer, 1, 1, me]))

    def diagonal_id(slot, role):
        return resident(pairs[me, slot, role, me])

    def window_step(window, d, sign):
        b, c = lax.rem(window, span), lax.div(window, span)
        dx, dy = lax.rem(d + b, span), lax.rem(d + c, span)
        if sign < 0:
            dx, dy, d = span - dx, span - dy, span - d
        px, py, pz = lax.rem(x + dx, span), lax.rem(y + dy, span), lax.rem(z + d, span)
        return (px * span + pz) * span + py, lax.rem(dx, 2)

    groups = chips // (2 * span)
    places = chips + 1
    block_sends, sib_sends, back_sends, diagonal_sends, gain_sends = (
        send_sem.at[k] for k in range(5)
    )

    def wait_bytes(ref, sem):
        pltpu.make_async_copy(ref, ref, sem).wait()

    def group_of(window):
        return arrive_sem.at[lax.div(window, 2)]

    def kept_role(peer):
        return jnp.where(peer < me, 1, 0)

    def block_copy(peer, core, window):
        role = jnp.where(peer > me, 0, 1)
        return remote(
            staged.at[peer], blocks.at[me, role, feat], block_sends, group_of(window),
            place(peer, core),
        )

    def label_copy(peer, core, window):
        return remote(
            labels_hbm.at[peer, 1, my_rows], labels.at[me, my_rows], label_send_sem.at[peer],
            group_of(window), place(peer, core),
        )

    def label_own(peer, slot, sem):
        return pltpu.make_async_copy(labels_hbm.at[peer, slot], labels.at[peer], sem)

    def sib_copy(peer, sem):
        return remote(
            staged_sib.at[peer], blocks.at[peer, kept_role(peer), feat], sib_sends, sem, sibling
        )

    def diagonal_col_copy():
        return remote(
            staged.at[me], blocks.at[me, 1, feat], block_sends, arrive_sem.at[groups], sibling
        )

    def back_copy(peer, half):
        return remote(
            grads.at[peer, 1 - kept_role(peer), half], terms.at[me], back_sends,
            term_sem.at[0], place(peer, half),
        )

    def keep_copy(peer):
        return remote(
            grads.at[peer, kept_role(peer), other], terms.at[places + peer], sib_sends,
            term_sem.at[1], sibling,
        )

    def keep_own(peer):
        return pltpu.make_async_copy(
            grads.at[peer, kept_role(peer), feat], terms.at[places + peer], term_sem.at[1]
        )

    def diagonal_copy(role):
        where = me if role == 0 else chips
        return remote(
            grads.at[me, role, other], terms.at[feat * places + where], diagonal_sends,
            term_sem.at[0], sibling,
        )

    def diagonal_own(role):
        where = me if role == 0 else chips
        return pltpu.make_async_copy(
            grads.at[me, role, feat], terms.at[feat * places + where], term_sem.at[1]
        )

    def each_peer(action, sign):
        def body(window, _):
            for d in range(span):
                peer, core = window_step(window, d, sign)
                if d == 0:
                    pl.when(peer != me)(functools.partial(action, peer, core, window))
                else:
                    action(peer, core, window)
            return 0

        lax.fori_loop(0, span * span, body, 0)

    emb_copy = pltpu.make_async_copy(emb_hbm, emb, entry_sem.at[0])
    pairs_copy = pltpu.make_async_copy(pairs_hbm, pairs, entry_sem.at[1])
    counts_copy = pltpu.make_async_copy(counts_hbm, counts, entry_sem.at[2])
    pairs_copy.start()
    emb_copy.start()
    counts_copy.start()
    barrier = pltpu.get_barrier_semaphore()
    pl.semaphore_signal(barrier, 1, device_id=sibling, device_id_type=MESH)

    def greet(peer, core, window):
        for core in range(2):
            pl.semaphore_signal(barrier, 1, device_id=place(peer, core), device_id_type=MESH)

    each_peer(greet, 1)
    gains[feat] = gain_ref[...]
    pairs_copy.wait()
    emb_copy.wait()

    staged_sib[me] = emb[diagonal_id(other, 0)]
    staged[me] = emb[diagonal_id(other, 1)]

    pl.semaphore_wait(barrier, 2 * chips - 1)
    gain_scale = remote(
        gain_ref, gains.at[feat], small_sem.at[0], small_sem.at[1], sibling
    )

    def send(peer, core, window):
        staged[peer] = emb[sent_id(peer)]
        block_copy(peer, core, window).start()

        @pl.when(peer > me)
        def _():
            label_copy(peer, core, window).start()

    each_peer(send, 1)

    gain_scale.start()
    sib_copy(me, arrive_sem.at[groups]).start()
    diagonal_col_copy().start()
    label_own(me, feat, arrive_sem.at[groups]).start()
    blocks[me, 0, feat] = emb[diagonal_id(feat, 0)]
    blocks[me, 1, feat] = emb[diagonal_id(feat, 1)]

    def keep(peer, core, window):
        @pl.when(core == other)
        def _():
            staged_sib[peer] = emb[kept_id(peer)]
            sib_copy(peer, group_of(window)).start()

        @pl.when(core == feat)
        def _():
            blocks[peer, kept_role(peer), feat] = emb[kept_id(peer)]

            @pl.when(peer > me)
            def _():
                label_own(peer, 0, group_of(window)).start()

    each_peer(keep, -1)

    def list_ids(peer, _):
        on_diagonal = peer == me
        ids_out[0, peer] = jnp.where(on_diagonal, diagonal_id(0, 0), sent_id(peer))
        ids_out[1, peer] = jnp.where(on_diagonal, diagonal_id(1, 0), kept_id(peer))
        return 0

    lax.fori_loop(0, chips, list_ids, 0)
    for slot in range(2):
        ids_out[slot, chips] = diagonal_id(slot, 1)
    counts_copy.wait()

    def live(peer):
        at_requester = jnp.where(counts[me, peer] > 0, 1.0, 0.0)
        at_owner = jnp.where(counts[peer, me] > 1, 1.0, 0.0)
        worked = jnp.where(peer > me, at_requester, at_owner)
        return jnp.where(peer == me, 0.0, worked)

    gain_scale.wait_recv()
    gain_pair = jnp.concatenate([gains[feat], gains[other]], axis=-1)

    def tile(peer, goes_to, is_live, gain_sum):
        rows = jnp.concatenate([blocks[peer, 0, feat], blocks[peer, 0, other]], axis=-1)
        col = jnp.concatenate([blocks[peer, 1, feat], blocks[peer, 1, other]], axis=-1)
        rows_wide = rows.astype(jnp.float32)
        scaled = (rows_wide * gain_pair).astype(jnp.bfloat16)
        logits = lax.dot_general(
            scaled, col, (((1,), (1,)), ((), ())), preferred_element_type=jnp.float32
        )
        prob = 0.5 * jnp.tanh(0.5 * logits) + 0.5
        residual = ((prob - labels[peer].astype(jnp.float32)) * is_live).astype(jnp.bfloat16)
        pulled = jnp.dot(residual, col, preferred_element_type=jnp.float32)
        row_term = (pulled * gain_pair).astype(jnp.bfloat16)
        col_term = lax.dot_general(
            residual, scaled, (((0,), (0,)), ((), ())), preferred_element_type=jnp.float32
        ).astype(jnp.bfloat16)
        grads[goes_to, 0, feat] = row_term[:, :width]
        grads[goes_to, 0, other] = row_term[:, width:]
        grads[goes_to, 1, feat] = col_term[:, :width]
        grads[goes_to, 1, other] = col_term[:, width:]
        product = rows_wide * pulled
        return gain_sum + jnp.sum(product.reshape(-1, 8, 2 * width), axis=0)

    wait_bytes(staged.at[pl.ds(0, 3)], arrive_sem.at[groups])
    gain_sum = tile(
        me, me, jnp.where(counts[me, me] > feat, 1.0, 0.0), jnp.zeros((8, 2 * width), jnp.float32)
    )
    for role in range(2):
        diagonal_copy(role).start()
        diagonal_own(role).start()

    def mine(group, j):
        window = 2 * group + j // (span // 2)
        d = lax.rem(feat + window, 2) + 2 * (j % (span // 2))
        return window_step(window, d, -1)[0]

    def work(group, gain_sum):
        peers = [mine(group, j) for j in range(span)]
        short = (group == 0) & (feat == 0)

        @pl.when(short)
        def _():
            wait_bytes(blocks.at[pl.ds(0, span - 1)], arrive_sem.at[0])

        @pl.when(jnp.logical_not(short))
        def _():
            wait_bytes(blocks.at[pl.ds(0, span)], arrive_sem.at[group])

        for peer in peers:
            gain_sum = tile(peer, jnp.where(peer == me, chips, peer), live(peer), gain_sum)
        for peer in peers:

            @pl.when(peer != me)
            def _(peer=peer):
                for half in range(2):
                    back_copy(peer, half).start()
                keep_copy(peer).start()
                keep_own(peer).start()

        return gain_sum

    gain_sum = lax.fori_loop(0, groups, work, gain_sum)

    gain_sum = jnp.sum(gain_sum, axis=0, keepdims=True)
    gain_send[0] = gain_sum[:, width:]
    gain_pairwise = remote(
        gain_send.at[0], gain_sib, small_sem.at[2], small_sem.at[3], sibling
    )
    gain_pairwise.start()
    gain_pairwise.wait_recv()
    chip_gain = gain_sum[:, :width] + gain_sib[...]
    gain_send[1] = chip_gain
    gain_all[me] = chip_gain

    def start_gain(peer, core, window):
        remote(
            gain_send.at[1], gain_all.at[me], gain_sends, small_sem.at[4], place(peer, feat)
        ).start()

    each_peer(start_gain, 1)

    wait_bytes(terms.at[pl.ds(places, places)], term_sem.at[1])
    wait_bytes(staged, block_sends)
    wait_bytes(staged, sib_sends)
    wait_bytes(grads.at[0, 0], diagonal_sends)
    half_peers = chips // 2

    @pl.when(feat == 0)
    def _():
        wait_bytes(grads.at[pl.ds(0, half_peers - 1), 0], back_sends)

    @pl.when(feat == 1)
    def _():
        wait_bytes(grads.at[pl.ds(0, half_peers), 0], back_sends)

    def drain_label(peer, core, window):
        @pl.when(peer > me)
        def _():
            label_copy(peer, core, window).wait_send()

    each_peer(drain_label, 1)
    wait_bytes(gain_all.at[pl.ds(0, chips - 1)], gain_sends)
    wait_bytes(gain_all.at[pl.ds(0, chips - 1)], small_sem.at[4])

    def add_gain(chip, total):
        return total + gain_all[chip]

    total = lax.fori_loop(0, chips, add_gain, jnp.zeros((1, width), jnp.float32))
    gain_out[...] = total * (16.0 / (chips * emb.shape[1]))

    wait_bytes(terms.at[pl.ds(0, places)], term_sem.at[0])
    gain_scale.wait_send()
    gain_pairwise.wait_send()


def add_kernel(ids, terms, gain_ref, out_hbm, gain_out, sums, head, following, out_sem):
    none = terms.shape[0]
    places = none // 2
    count = sums.shape[0]
    piece = count // PIECES

    def copy_out(k):
        span = pl.ds(k * piece, piece)
        return pltpu.make_async_copy(sums.at[span], out_hbm.at[span], out_sem.at[k])

    gain_out[...] = gain_ref[...]
    following[none] = none

    def clear(step, _):
        for j in range(4):
            head[step * 4 + j] = none
        return 0

    lax.fori_loop(0, count // 4, clear, 0)

    def link(place, _):
        for slot in range(2):
            term = slot * places + place
            block = ids[slot, place]
            following[term] = head[block]
            head[block] = term
        return 0

    lax.fori_loop(0, places, link, 0)

    def term_or_zero(t):
        return jnp.where(t < none, terms[jnp.minimum(t, none - 1)].astype(jnp.float32), 0.0)

    def four(step, _):
        blocks = [step * 4 + j for j in range(4)]
        first = [head[b] for b in blocks]
        second = [following[t] for t in first]
        third = [following[t] for t in second]
        for b, t, u in zip(blocks, first, second):
            sums[b] = term_or_zero(t) + term_or_zero(u)
        least = jnp.minimum(jnp.minimum(third[0], third[1]), jnp.minimum(third[2], third[3]))

        @pl.when(least < none)
        def _():
            for b, t in zip(blocks, third):

                def rest(t, b=b):
                    sums[b] += terms[t].astype(jnp.float32)
                    return following[t]

                lax.while_loop(lambda t: t < none, rest, t)

        return 0

    def one_piece(k, _):
        lax.fori_loop(k * (piece // 4), (k + 1) * (piece // 4), four, 0)
        copy_out(k).start()
        return 0

    lax.fori_loop(0, PIECES, one_piece, 0)

    def finish(k, _):
        copy_out(k).wait()
        return 0

    lax.fori_loop(0, PIECES, finish, 0)


def local(embeddings, decoder_gain, block_pairs, pair_counts, edge_labels):
    span = lax.axis_size("partner")
    chips = lax.axis_size("row") * span
    tile = edge_labels.shape[-1]
    width = embeddings.shape[1]
    count = embeddings.shape[0] // tile
    resident = embeddings.reshape(count, tile, width)
    labels = edge_labels.reshape(chips, 2, tile, tile)
    pairs = block_pairs.transpose(0, 2, 3, 1)

    smem = pl.BlockSpec(memory_space=pltpu.SMEM)
    vmem = pl.BlockSpec(memory_space=pltpu.VMEM)
    anywhere = pl.BlockSpec(memory_space=pl.ANY)
    dma = pltpu.SemaphoreType.DMA
    half = jnp.bfloat16
    terms, gain_total, ids = pl.pallas_call(
        functools.partial(exchange_kernel, chips, span),
        out_shape=(
            pltpu.VMEM((2 * (chips + 1), tile, width), half),
            pltpu.VMEM((1, width), jnp.float32),
            pltpu.SMEM((2, chips + 1), jnp.int32),
        ),
        in_specs=[vmem, anywhere, anywhere, anywhere, anywhere],
        out_specs=(vmem, vmem, smem),
        scratch_shapes=[
            pltpu.SMEM((chips, 2, 2, chips), jnp.int32),
            pltpu.SMEM((chips, chips), jnp.int32),
            pltpu.VMEM((count, tile, width), half),
            pltpu.VMEM((chips, tile, width), half),
            pltpu.VMEM((chips, tile, width), half),
            pltpu.VMEM((chips, 2, 2, tile, width), half),
            pltpu.VMEM((chips, tile, tile), half),
            pltpu.VMEM((chips + 1, 2, 2, tile, width), half),
            pltpu.VMEM((2, 1, width), jnp.float32),
            pltpu.VMEM((2, 1, width), jnp.float32),
            pltpu.VMEM((1, width), jnp.float32),
            pltpu.VMEM((chips, 1, width), jnp.float32),
            dma((3,)),
            dma((chips // (2 * span) + 1,)),
            dma((chips,)),
            dma((5,)),
            dma((2,)),
            dma((5,)),
        ],
        compiler_params=pltpu.CompilerParams(
            collective_id=0, has_side_effects=True, vmem_limit_bytes=56 * 2**20
        ),
        name="exchange",
    )(
        decoder_gain.reshape(1, width),
        *(
            pltpu.with_memory_space_constraint(array, pltpu.HBM)
            for array in (pairs, pair_counts, resident, labels)
        ),
    )

    places = 2 * (chips + 1)
    grad, gain = pl.pallas_call(
        add_kernel,
        in_specs=[smem, vmem, vmem],
        out_specs=(anywhere, vmem),
        out_shape=(
            jax.ShapeDtypeStruct((count, tile, width), jnp.float32),
            jax.ShapeDtypeStruct((1, width), jnp.float32),
        ),
        scratch_shapes=[
            pltpu.VMEM((count, tile, width), jnp.float32),
            pltpu.SMEM((count,), jnp.int32),
            pltpu.SMEM((places + 1,), jnp.int32),
            dma((PIECES,)),
        ],
        compiler_params=pltpu.CompilerParams(vmem_limit_bytes=48 * 2**20),
        name="add_terms",
    )(
        pltpu.with_memory_space_constraint(ids, pltpu.SMEM),
        pltpu.with_memory_space_constraint(terms, pltpu.VMEM),
        pltpu.with_memory_space_constraint(gain_total, pltpu.VMEM),
    )
    return grad.reshape(count * tile, width), gain.reshape(width)


def solution(mesh):
    in_specs = (
        P(("row", "partner"), "feat"),
        P("feat"),
        P(),
        P(),
        P(("row", "partner"), None, None, None, None),
    )
    out_specs = (P(("row", "partner"), "feat"), P("feat"))
    return jax.shard_map(local, mesh=mesh, in_specs=in_specs, out_specs=out_specs, check_vma=False)
```

```python
import functools

import jax
import jax.numpy as jnp
from jax import lax
from jax.experimental import pallas as pl
from jax.experimental.pallas import tpu as pltpu
from jax.sharding import PartitionSpec as P

PIECES = 8
MESH = pl.DeviceIdType.MESH


def exchange_kernel(
    chips,
    span,
    gain_ref,
    pairs_hbm,
    counts_hbm,
    emb_hbm,
    labels_hbm,
    terms,
    gain_out,
    ids_out,
    pairs,
    counts,
    emb,
    staged,
    staged_sib,
    blocks,
    labels,
    grads,
    gains,
    gain_send,
    gain_sib,
    gain_all,
    entry_sem,
    arrive_sem,
    label_send_sem,
    send_sem,
    term_sem,
    small_sem,
):
    row = lax.axis_index("row")
    x, y, z = row // span, lax.axis_index("partner"), row % span
    me = row * span + y
    feat = lax.axis_index("feat")
    other = 1 - feat
    width = emb.shape[-1]
    half_rows = labels.shape[1] // 2
    my_rows = pl.ds(pl.multiple_of(feat * half_rows, half_rows), half_rows)

    def place(chip, core):
        return (chip // span, chip % span, core)

    sibling = place(me, other)

    def remote(src, dst, send, recv, where):
        return pltpu.make_async_remote_copy(
            src_ref=src, dst_ref=dst, send_sem=send, recv_sem=recv,
            device_id=where, device_id_type=MESH,
        )

    count = emb.shape[0]
    base = me * count

    def resident(block):
        return jnp.clip(block - base, 0, count - 1)

    def sent_id(peer):
        return resident(jnp.where(peer > me, pairs[me, 1, 0, peer], pairs[peer, 0, 1, me]))

    def kept_id(peer):
        return resident(jnp.where(peer > me, pairs[me, 0, 0, peer], pairs[peer, 1, 1, me]))

    def diagonal_id(slot, role):
        return resident(pairs[me, slot, role, me])

    def window_step(window, d, sign):
        b, c = lax.rem(window, span), lax.div(window, span)
        dx, dy = lax.rem(d + b, span), lax.rem(d + c, span)
        if sign < 0:
            dx, dy, d = span - dx, span - dy, span - d
        px, py, pz = lax.rem(x + dx, span), lax.rem(y + dy, span), lax.rem(z + d, span)
        return (px * span + pz) * span + py, lax.rem(dx, 2)

    groups = chips // (2 * span)
    places = chips + 1
    block_sends, sib_sends, back_sends, diagonal_sends, gain_sends = (
        send_sem.at[k] for k in range(5)
    )

    def wait_bytes(ref, sem):
        pltpu.make_async_copy(ref, ref, sem).wait()

    def group_of(window):
        return arrive_sem.at[lax.div(window, 2)]

    def kept_role(peer):
        return jnp.where(peer < me, 1, 0)

    def block_copy(peer, core, window):
        role = jnp.where(peer > me, 0, 1)
        return remote(
            staged.at[peer], blocks.at[me, role, feat], block_sends, group_of(window),
            place(peer, core),
        )

    def label_copy(peer, core, window):
        return remote(
            labels_hbm.at[peer, 1, my_rows], labels.at[me, my_rows], label_send_sem.at[peer],
            group_of(window), place(peer, core),
        )

    def label_own(peer, slot, sem):
        return pltpu.make_async_copy(labels_hbm.at[peer, slot], labels.at[peer], sem)

    def sib_copy(peer, sem):
        return remote(
            staged_sib.at[peer], blocks.at[peer, kept_role(peer), feat], sib_sends, sem, sibling
        )

    def diagonal_col_copy():
        return remote(
            staged.at[me], blocks.at[me, 1, feat], block_sends, arrive_sem.at[groups], sibling
        )

    def back_copy(peer, half):
        return remote(
            grads.at[peer, 1 - kept_role(peer), half], terms.at[me], back_sends,
            term_sem.at[0], place(peer, half),
        )

    def keep_copy(peer):
        return remote(
            grads.at[peer, kept_role(peer), other], terms.at[places + peer], sib_sends,
            term_sem.at[1], sibling,
        )

    def keep_own(peer):
        return pltpu.make_async_copy(
            grads.at[peer, kept_role(peer), feat], terms.at[places + peer], term_sem.at[1]
        )

    def diagonal_copy(role):
        where = me if role == 0 else chips
        return remote(
            grads.at[me, role, other], terms.at[feat * places + where], diagonal_sends,
            term_sem.at[0], sibling,
        )

    def diagonal_own(role):
        where = me if role == 0 else chips
        return pltpu.make_async_copy(
            grads.at[me, role, feat], terms.at[feat * places + where], term_sem.at[1]
        )

    def each_peer(action, sign):
        def body(window, _):
            for d in range(span):
                peer, core = window_step(window, d, sign)
                if d == 0:
                    pl.when(peer != me)(functools.partial(action, peer, core, window))
                else:
                    action(peer, core, window)
            return 0

        lax.fori_loop(0, span * span, body, 0)

    emb_copy = pltpu.make_async_copy(emb_hbm, emb, entry_sem.at[0])
    pairs_copy = pltpu.make_async_copy(pairs_hbm, pairs, entry_sem.at[1])
    counts_copy = pltpu.make_async_copy(counts_hbm, counts, entry_sem.at[2])
    pairs_copy.start()
    emb_copy.start()
    counts_copy.start()
    barrier = pltpu.get_barrier_semaphore()
    pl.semaphore_signal(barrier, 1, device_id=sibling, device_id_type=MESH)

    def greet(peer, core, window):
        for core in range(2):
            pl.semaphore_signal(barrier, 1, device_id=place(peer, core), device_id_type=MESH)

    each_peer(greet, 1)
    gains[feat] = gain_ref[...]
    pairs_copy.wait()
    emb_copy.wait()

    staged_sib[me] = emb[diagonal_id(other, 0)]
    staged[me] = emb[diagonal_id(other, 1)]

    pl.semaphore_wait(barrier, 2 * chips - 1)
    gain_scale = remote(
        gain_ref, gains.at[feat], small_sem.at[0], small_sem.at[1], sibling
    )

    def send(peer, core, window):
        staged[peer] = emb[sent_id(peer)]
        block_copy(peer, core, window).start()

        @pl.when(peer > me)
        def _():
            label_copy(peer, core, window).start()

    each_peer(send, 1)

    gain_scale.start()
    sib_copy(me, arrive_sem.at[groups]).start()
    diagonal_col_copy().start()
    label_own(me, feat, arrive_sem.at[groups]).start()
    blocks[me, 0, feat] = emb[diagonal_id(feat, 0)]
    blocks[me, 1, feat] = emb[diagonal_id(feat, 1)]

    def keep(peer, core, window):
        @pl.when(core == other)
        def _():
            staged_sib[peer] = emb[kept_id(peer)]
            sib_copy(peer, group_of(window)).start()

        @pl.when(core == feat)
        def _():
            blocks[peer, kept_role(peer), feat] = emb[kept_id(peer)]

            @pl.when(peer > me)
            def _():
                label_own(peer, 0, group_of(window)).start()

    each_peer(keep, -1)

    def list_ids(peer, _):
        on_diagonal = peer == me
        ids_out[0, peer] = jnp.where(on_diagonal, diagonal_id(0, 0), sent_id(peer))
        ids_out[1, peer] = jnp.where(on_diagonal, diagonal_id(1, 0), kept_id(peer))
        return 0

    lax.fori_loop(0, chips, list_ids, 0)
    for slot in range(2):
        ids_out[slot, chips] = diagonal_id(slot, 1)
    counts_copy.wait()

    def live(peer):
        at_requester = jnp.where(counts[me, peer] > 0, 1.0, 0.0)
        at_owner = jnp.where(counts[peer, me] > 1, 1.0, 0.0)
        worked = jnp.where(peer > me, at_requester, at_owner)
        return jnp.where(peer == me, 0.0, worked)

    gain_scale.wait_recv()
    gain_pair = jnp.concatenate([gains[feat], gains[other]], axis=-1)

    def tile(peer, goes_to, is_live, gain_sum):
        rows = jnp.concatenate([blocks[peer, 0, feat], blocks[peer, 0, other]], axis=-1)
        col = jnp.concatenate([blocks[peer, 1, feat], blocks[peer, 1, other]], axis=-1)
        rows_wide = rows.astype(jnp.float32)
        scaled = (rows_wide * gain_pair).astype(jnp.bfloat16)
        logits = lax.dot_general(
            scaled, col, (((1,), (1,)), ((), ())), preferred_element_type=jnp.float32
        )
        prob = 0.5 * jnp.tanh(0.5 * logits) + 0.5
        residual = ((prob - labels[peer].astype(jnp.float32)) * is_live).astype(jnp.bfloat16)
        pulled = jnp.dot(residual, col, preferred_element_type=jnp.float32)
        row_term = (pulled * gain_pair).astype(jnp.bfloat16)
        col_term = lax.dot_general(
            residual, scaled, (((0,), (0,)), ((), ())), preferred_element_type=jnp.float32
        ).astype(jnp.bfloat16)
        grads[goes_to, 0, feat] = row_term[:, :width]
        grads[goes_to, 0, other] = row_term[:, width:]
        grads[goes_to, 1, feat] = col_term[:, :width]
        grads[goes_to, 1, other] = col_term[:, width:]
        product = rows_wide * pulled
        return gain_sum + jnp.sum(product.reshape(-1, 8, 2 * width), axis=0)

    wait_bytes(staged.at[pl.ds(0, 3)], arrive_sem.at[groups])
    gain_sum = tile(
        me, me, jnp.where(counts[me, me] > feat, 1.0, 0.0), jnp.zeros((8, 2 * width), jnp.float32)
    )
    for role in range(2):
        diagonal_copy(role).start()
        diagonal_own(role).start()

    def mine(group, j):
        window = 2 * group + j // (span // 2)
        d = lax.rem(feat + window, 2) + 2 * (j % (span // 2))
        return window_step(window, d, -1)[0]

    def work(group, gain_sum):
        peers = [mine(group, j) for j in range(span)]
        short = (group == 0) & (feat == 0)

        @pl.when(short)
        def _():
            wait_bytes(blocks.at[pl.ds(0, span - 1)], arrive_sem.at[0])

        @pl.when(jnp.logical_not(short))
        def _():
            wait_bytes(blocks.at[pl.ds(0, span)], arrive_sem.at[group])

        for peer in peers:
            gain_sum = tile(peer, jnp.where(peer == me, chips, peer), live(peer), gain_sum)
        return gain_sum

    def give_back(group):
        for peer in [mine(group, j) for j in range(span)]:

            @pl.when(peer != me)
            def _(peer=peer):
                for half in range(2):
                    back_copy(peer, half).start()
                keep_copy(peer).start()
                keep_own(peer).start()

    def work_and_give(group, gain_sum):
        gain_sum = work(group, gain_sum)
        give_back(group)
        return gain_sum

    last = jnp.int32(groups - 1)
    gain_sum = lax.fori_loop(0, groups - 1, work_and_give, gain_sum)
    gain_sum = work(last, gain_sum)

    gain_sum = jnp.sum(gain_sum, axis=0, keepdims=True)
    gain_send[0] = gain_sum[:, width:]
    gain_pairwise = remote(
        gain_send.at[0], gain_sib, small_sem.at[2], small_sem.at[3], sibling
    )
    gain_pairwise.start()
    give_back(last)
    gain_pairwise.wait_recv()
    chip_gain = gain_sum[:, :width] + gain_sib[...]
    gain_send[1] = chip_gain
    gain_all[me] = chip_gain

    def start_gain(peer, core, window):
        remote(
            gain_send.at[1], gain_all.at[me], gain_sends, small_sem.at[4], place(peer, feat)
        ).start()

    each_peer(start_gain, 1)

    wait_bytes(terms.at[pl.ds(places, places)], term_sem.at[1])
    wait_bytes(staged, block_sends)
    wait_bytes(staged, sib_sends)
    wait_bytes(grads.at[0, 0], diagonal_sends)
    half_peers = chips // 2

    @pl.when(feat == 0)
    def _():
        wait_bytes(grads.at[pl.ds(0, half_peers - 1), 0], back_sends)

    @pl.when(feat == 1)
    def _():
        wait_bytes(grads.at[pl.ds(0, half_peers), 0], back_sends)

    def drain_label(peer, core, window):
        @pl.when(peer > me)
        def _():
            label_copy(peer, core, window).wait_send()

    each_peer(drain_label, 1)
    wait_bytes(gain_all.at[pl.ds(0, chips - 1)], gain_sends)
    wait_bytes(gain_all.at[pl.ds(0, chips - 1)], small_sem.at[4])

    def add_gain(chip, total):
        return total + gain_all[chip]

    total = lax.fori_loop(0, chips, add_gain, jnp.zeros((1, width), jnp.float32))
    gain_out[...] = total * (16.0 / (chips * emb.shape[1]))

    wait_bytes(terms.at[pl.ds(0, places)], term_sem.at[0])
    gain_scale.wait_send()
    gain_pairwise.wait_send()


def add_kernel(ids, terms, gain_ref, out_hbm, gain_out, sums, head, following, out_sem):
    none = terms.shape[0]
    places = none // 2
    count = sums.shape[0]
    piece = count // PIECES

    def copy_out(k):
        span = pl.ds(k * piece, piece)
        return pltpu.make_async_copy(sums.at[span], out_hbm.at[span], out_sem.at[k])

    gain_out[...] = gain_ref[...]
    following[none] = none

    def clear(step, _):
        for j in range(4):
            head[step * 4 + j] = none
        return 0

    lax.fori_loop(0, count // 4, clear, 0)

    unroll = 5 if places % 5 == 0 else 1

    def link(step, _):
        for j in range(unroll):
            place = step * unroll + j
            for slot in range(2):
                term = slot * places + place
                block = ids[slot, place]
                following[term] = head[block]
                head[block] = term
        return 0

    lax.fori_loop(0, places // unroll, link, 0)

    def term_or_zero(t):
        return jnp.where(t < none, terms[jnp.minimum(t, none - 1)].astype(jnp.float32), 0.0)

    def four(step, _):
        blocks = [step * 4 + j for j in range(4)]
        first = [head[b] for b in blocks]
        second = [following[t] for t in first]
        third = [following[t] for t in second]
        for b, t, u in zip(blocks, first, second):
            sums[b] = term_or_zero(t) + term_or_zero(u)
        least = jnp.minimum(jnp.minimum(third[0], third[1]), jnp.minimum(third[2], third[3]))

        @pl.when(least < none)
        def _():
            for b, t in zip(blocks, third):

                def rest(t, b=b):
                    sums[b] += terms[t].astype(jnp.float32)
                    return following[t]

                lax.while_loop(lambda t: t < none, rest, t)

        return 0

    def one_piece(k, _):
        lax.fori_loop(k * (piece // 4), (k + 1) * (piece // 4), four, 0)
        copy_out(k).start()
        return 0

    lax.fori_loop(0, PIECES, one_piece, 0)

    def finish(k, _):
        copy_out(k).wait()
        return 0

    lax.fori_loop(0, PIECES, finish, 0)


def local(embeddings, decoder_gain, block_pairs, pair_counts, edge_labels):
    span = lax.axis_size("partner")
    chips = lax.axis_size("row") * span
    tile = edge_labels.shape[-1]
    width = embeddings.shape[1]
    count = embeddings.shape[0] // tile
    resident = embeddings.reshape(count, tile, width)
    labels = edge_labels.reshape(chips, 2, tile, tile)
    pairs = block_pairs.transpose(0, 2, 3, 1)

    smem = pl.BlockSpec(memory_space=pltpu.SMEM)
    vmem = pl.BlockSpec(memory_space=pltpu.VMEM)
    anywhere = pl.BlockSpec(memory_space=pl.ANY)
    dma = pltpu.SemaphoreType.DMA
    half = jnp.bfloat16
    terms, gain_total, ids = pl.pallas_call(
        functools.partial(exchange_kernel, chips, span),
        out_shape=(
            pltpu.VMEM((2 * (chips + 1), tile, width), half),
            pltpu.VMEM((1, width), jnp.float32),
            pltpu.SMEM((2, chips + 1), jnp.int32),
        ),
        in_specs=[vmem, anywhere, anywhere, anywhere, anywhere],
        out_specs=(vmem, vmem, smem),
        scratch_shapes=[
            pltpu.SMEM((chips, 2, 2, chips), jnp.int32),
            pltpu.SMEM((chips, chips), jnp.int32),
            pltpu.VMEM((count, tile, width), half),
            pltpu.VMEM((chips, tile, width), half),
            pltpu.VMEM((chips, tile, width), half),
            pltpu.VMEM((chips, 2, 2, tile, width), half),
            pltpu.VMEM((chips, tile, tile), half),
            pltpu.VMEM((chips + 1, 2, 2, tile, width), half),
            pltpu.VMEM((2, 1, width), jnp.float32),
            pltpu.VMEM((2, 1, width), jnp.float32),
            pltpu.VMEM((1, width), jnp.float32),
            pltpu.VMEM((chips, 1, width), jnp.float32),
            dma((3,)),
            dma((chips // (2 * span) + 1,)),
            dma((chips,)),
            dma((5,)),
            dma((2,)),
            dma((5,)),
        ],
        compiler_params=pltpu.CompilerParams(
            collective_id=0, has_side_effects=True, vmem_limit_bytes=56 * 2**20
        ),
        name="exchange",
    )(
        decoder_gain.reshape(1, width),
        *(
            pltpu.with_memory_space_constraint(array, pltpu.HBM)
            for array in (pairs, pair_counts, resident, labels)
        ),
    )

    places = 2 * (chips + 1)
    grad, gain = pl.pallas_call(
        add_kernel,
        in_specs=[smem, vmem, vmem],
        out_specs=(anywhere, vmem),
        out_shape=(
            jax.ShapeDtypeStruct((count, tile, width), jnp.float32),
            jax.ShapeDtypeStruct((1, width), jnp.float32),
        ),
        scratch_shapes=[
            pltpu.VMEM((count, tile, width), jnp.float32),
            pltpu.SMEM((count,), jnp.int32),
            pltpu.SMEM((places + 1,), jnp.int32),
            dma((PIECES,)),
        ],
        compiler_params=pltpu.CompilerParams(vmem_limit_bytes=48 * 2**20),
        name="add_terms",
    )(
        pltpu.with_memory_space_constraint(ids, pltpu.SMEM),
        pltpu.with_memory_space_constraint(terms, pltpu.VMEM),
        pltpu.with_memory_space_constraint(gain_total, pltpu.VMEM),
    )
    return grad.reshape(count * tile, width), gain.reshape(width)


def solution(mesh):
    in_specs = (
        P(("row", "partner"), "feat"),
        P("feat"),
        P(),
        P(),
        P(("row", "partner"), None, None, None, None),
    )
    out_specs = (P(("row", "partner"), "feat"), P("feat"))
    return jax.shard_map(local, mesh=mesh, in_specs=in_specs, out_specs=out_specs, check_vma=False)
```
